32 devices in a mesh: fsdp: 4 (over x, core), dp: 8 (over z, y).
Axes of the slice: x: 2, y: 2, z: 4, core: 2. Of those that a mesh axis runs over, the one named last changes fastest.
Arguments:
- block_input: bfloat16 [8, 1024, 768], P('dp', 'fsdp'), may hold values from -6 to 6
- out_cotangent: bfloat16 [8, 1024, 768], P('dp', 'fsdp'), may hold values from -6 to 6
- doc_lengths: int32 [8, 4], P('dp'), may hold values from 1 to 1021, as said below
- norm_gain: bfloat16 [768], P('fsdp'), may hold values from 0.5 to 1.5
- in_weight: bfloat16 [768, 3352], P('fsdp'), may hold values from -0.21875 to 0.21875
- conv_weight: bfloat16 [4, 1792], P(None, 'fsdp'), may hold values from -3 to 3
- conv_bias: bfloat16 [1792], P('fsdp'), may hold values from -2 to 2
- step_bias: bfloat16 [24], P('fsdp'), may hold values from -6.5 to -2.1875
- decay_log: bfloat16 [24], P('fsdp'), may hold values from -4.5 to 1
- skip_gain: bfloat16 [24], P('fsdp'), may hold values from 0.5 to 1.5
- out_gain: bfloat16 [1536], P('fsdp'), may hold values from 0.5 to 1.5
- out_weight: bfloat16 [1536, 768], P('fsdp'), may hold values from -0.15625 to 0.15625
Outputs:
- block_output: bfloat16 [8, 1024, 768], P('dp', 'fsdp')
- input_grad: bfloat16 [8, 1024, 768], P('dp', 'fsdp')
- grad_norm_gain: float32 [768], P('fsdp')
- grad_in_weight: float32 [768, 3352], P('fsdp')
- grad_conv_weight: float32 [4, 1792], P(None, 'fsdp')
- grad_conv_bias: float32 [1792], P('fsdp')
- grad_step_bias: float32 [24], P('fsdp')
- grad_decay_log: float32 [24], P('fsdp')
- grad_skip_gain: float32 [24], P('fsdp')
- grad_out_gain: float32 [1536], P('fsdp')
- grad_out_weight: float32 [1536, 768], P('fsdp')
The draws below stay inside these ranges and needn't reach their ends.
Inputs may be any that keep to these rules, and one draw needn't show every extreme that they name: `doc_lengths`: row q lists the lengths of the 4 documents packed, in order, into sequence q, summing to 1024: the first ends within the sequence's first 256 positions and the last two begin within its last 256 positions.
All inputs are finite; a program needn't handle non-finite values.
Results may differ from the reference program's by a relative error of at most 0.019.
Values may be sent and summed in bfloat16 or wider, within the bound.
No kernel may reach another device: no remote copies, remote signals or barrier semaphores. Data moves between devices by JAX's collectives and lax.ppermute only.
A program may use at most 128 MiB of HBM per device.

```python
import jax
import jax.numpy as jnp
from jax import lax

D = 768
H = 24
P_SIZE = 64
N = 128
KCONV = 4
BLOCK = 256
TOK_SEQ = 256
DI = 1536
CONVCH = 1792
PROJ = 3352
SEQLEN = 1024
NSEQ = 8


def split_lengths(row_key):
    first_key, tail_key = jax.random.split(row_key)
    first_cut = jax.random.randint(first_key, (1,), 1, TOK_SEQ).astype(jnp.int32)
    tail_cuts = jnp.sort(jax.random.permutation(tail_key, TOK_SEQ - 1)[:2]).astype(jnp.int32) + (SEQLEN - TOK_SEQ + 1)
    edges = jnp.concatenate([jnp.zeros((1,), jnp.int32), first_cut, tail_cuts, jnp.full((1,), SEQLEN, jnp.int32)])
    return (edges[1:] - edges[:-1]).astype(jnp.int32)


def draw_doc_lengths(key, part):
    key = jax.random.fold_in(key, 7)
    row_keys = jax.random.split(key, NSEQ + 1)
    packed = jax.vmap(split_lengths)(row_keys[1:])
    chosen = jax.random.randint(row_keys[0], (), 0, NSEQ)
    extreme = jnp.array([1, SEQLEN - 3, 1, 1], jnp.int32)
    row_index = jnp.arange(NSEQ, dtype=jnp.int32)
    return jnp.where((row_index == chosen)[:, None], extreme[None, :], packed).astype(jnp.int32)


def levels(key, shape, cuts, smallest, high):
    level = 1.0
    for axis_at, parts in cuts:
        draws = jax.random.uniform(jax.random.fold_in(jax.random.fold_in(key, 6), axis_at), (parts,), jnp.float32, smallest / len(cuts), high / len(cuts))
        level = level * jnp.repeat(jnp.exp(draws), shape[axis_at] // parts).reshape((-1,) + (1,) * (len(shape) - 1 - axis_at))
    return level


def noise(own_key, shape, width, most, cuts=(), held_as=jnp.bfloat16):
    values = width * jax.random.normal(own_key, shape, jnp.float32)
    if cuts:
        values = values * levels(own_key, shape, cuts, -0.22, 0.18)
    return jnp.clip(values, -most, most).astype(held_as)


def setup_inputs(seed: int = 0) -> dict:
    streams_of = jax.random.split(jax.random.key(seed), 13)
    return {
        "block_input": noise(streams_of[0], (NSEQ, SEQLEN, D), 1.0, 6.0, ((0, 8), (1, 4))),
        "out_cotangent": noise(streams_of[1], (NSEQ, SEQLEN, D), 1.0, 6.0, ((0, 8), (1, 4))),
        "doc_lengths": draw_doc_lengths(jax.random.fold_in(streams_of[12], 71), 0),
        "norm_gain": jnp.clip(1.0 + 0.1 * jax.random.normal(streams_of[3], (D,), jnp.float32), 0.5, 1.5).astype(jnp.bfloat16),
        "in_weight": noise(streams_of[4], (D, PROJ), D ** -0.5, 0.21875, ((0, 4),)),
        "conv_weight": noise(streams_of[5], (KCONV, CONVCH), KCONV ** -0.5, 3.0, ((1, 4),)),
        "conv_bias": noise(streams_of[6], (CONVCH,), 0.3, 2.0, ((0, 4),)),
        "step_bias": jnp.clip(-6.5 + 4.3125 * jax.random.uniform(streams_of[7], (H,), jnp.float32) ** levels(streams_of[7], (H,), ((0, 4),), -0.2, 0.2), -6.5, -2.1875).astype(jnp.bfloat16),
        "decay_log": jnp.clip(-4.5 + 5.5 * jax.random.uniform(streams_of[8], (H,), jnp.float32) ** levels(streams_of[8], (H,), ((0, 4),), -0.2, 0.2), -4.5, 1.0).astype(jnp.bfloat16),
        "skip_gain": jnp.clip(0.5 + 1.0 * jax.random.uniform(streams_of[9], (H,), jnp.float32) ** levels(streams_of[9], (H,), ((0, 4),), -0.2, 0.2), 0.5, 1.5).astype(jnp.bfloat16),
        "out_gain": jnp.clip(1.0 + 0.1 * jax.random.normal(streams_of[10], (DI,), jnp.float32), 0.5, 1.5).astype(jnp.bfloat16),
        "out_weight": noise(streams_of[11], (DI, D), DI ** -0.5, 0.15625, ((0, 4),)),
    }


EPSILON = 1e-05
HIGHEST = lax.Precision.HIGHEST

@jax.custom_vjp
def low(v):
    return lax.optimization_barrier(v.astype(jnp.bfloat16)).astype(jnp.float32)

@jax.custom_vjp
def low_back(v):
    return v

def low_keep(v):
    return (low(v), None)

def low_pass(kept, grad):
    return (grad,)

def back_keep(v):
    return (v, None)

def back_low(kept, grad):
    return (low(grad),)
low.defvjp(low_keep, low_pass)
low_back.defvjp(back_keep, back_low)

def lower_tri(length):
    rows_iota = lax.broadcasted_iota(jnp.int32, (length, length), 0)
    cols_iota = lax.broadcasted_iota(jnp.int32, (length, length), 1)
    return (rows_iota >= cols_iota).astype(jnp.float32)

def block_terms(log_decay, segment, seg_before):
    length = segment.shape[0]
    lower_mask = lower_tri(length)
    cumulative = jnp.dot(lower_mask, log_decay, precision=HIGHEST)
    same_mask = lower_mask * (segment[:, None] == segment[None, :]).astype(jnp.float32)
    differences = cumulative.T[:, :, None] - cumulative.T[:, None, :]
    decay_table = jnp.exp(jnp.where(same_mask[None] > 0, differences, 0.0)) * same_mask[None]
    enter_rate = jnp.exp(cumulative) * (segment == seg_before).astype(jnp.float32)[:, None]
    tail_sum = cumulative[-1]
    same_last = (segment == segment[-1]).astype(jnp.float32)
    end_decay = jnp.exp(tail_sum[None, :] - cumulative) * same_last[:, None]
    keep_rate = jnp.exp(tail_sum) * (segment[-1] == seg_before).astype(jnp.float32)
    return (decay_table, enter_rate, end_decay, keep_rate)

def block_step(state, fields):
    heads_full, heads_low, keys_low, query_low, step_size, log_decay, segment, seg_before = fields
    decay_table, enter_rate, end_decay, keep_rate = block_terms(log_decay, segment, seg_before)
    gram_matrix = low_back(jnp.dot(query_low, keys_low.T, precision=HIGHEST))
    step_row = step_size.T[:, None, :]
    weights = low(gram_matrix[None] * decay_table * step_row)
    intra_out = jnp.einsum('hts,shp->thp', weights, heads_low, precision=HIGHEST)
    start_low = low(state)
    inter_out = jnp.einsum('tn,hpn->thp', query_low, start_low, precision=HIGHEST) * enter_rate[:, :, None]
    ssm_out = low_back(intra_out + inter_out)
    weighted = low(heads_full * (end_decay * step_size)[:, :, None])
    local_state = low_back(jnp.einsum('shp,sn->hpn', weighted, keys_low, precision=HIGHEST))
    new_state = keep_rate[:, None, None] * state + local_state
    return (new_state, ssm_out)

def segments_of(lengths_row, length):
    bounds = jnp.cumsum(lengths_row).astype(jnp.int32)[:-1]
    positions = jnp.arange(length, dtype=jnp.int32)
    return lax.optimization_barrier(jnp.sum((positions[:, None] >= bounds[None, :]).astype(jnp.int32), axis=1)).astype(jnp.int32)

def block(params, inputs, segment):
    gain_in, weight_in, conv_taps, conv_offset, step_bias, decay_log, skip_gain, gain_out, weight_out = params
    length = inputs.shape[0]
    scale_in = lax.rsqrt(lax.optimization_barrier(jnp.mean(inputs * inputs, axis=-1, keepdims=True)) + EPSILON)
    normed = low(inputs * scale_in * gain_in)
    projected = low(low_back(jnp.dot(normed, weight_in, precision=HIGHEST)))
    conv_part = projected[:, DI:DI + CONVCH]
    conv_input = jnp.concatenate([jnp.zeros((KCONV - 1, CONVCH), jnp.float32), conv_part], axis=0)
    segment_ext = jnp.concatenate([jnp.full((KCONV - 1,), -1, jnp.int32), segment])
    pre_act = jnp.broadcast_to(conv_offset, (length, CONVCH))
    for offset in range(KCONV):
        same_doc = (segment_ext[offset:offset + length] == segment).astype(jnp.float32)
        pre_act = pre_act + conv_taps[offset] * conv_input[offset:offset + length] * same_doc[:, None]
    activated = jax.nn.silu(pre_act)
    act_low = low(activated)
    blocks = length // BLOCK
    heads_full = activated[:, :DI].reshape(length, H, P_SIZE)
    step_size = jax.nn.softplus(projected[:, DI + CONVCH:] + step_bias)
    rate_values = -jnp.exp(decay_log)
    log_decay = step_size * rate_values
    seg_before = jnp.concatenate([jnp.full((1,), -1, jnp.int32), segment[BLOCK - 1::BLOCK][:-1]])
    fields = (heads_full.reshape(blocks, BLOCK, H, P_SIZE), act_low[:, :DI].reshape(blocks, BLOCK, H, P_SIZE), act_low[:, DI:DI + N].reshape(blocks, BLOCK, N), act_low[:, DI + N:].reshape(blocks, BLOCK, N), step_size.reshape(blocks, BLOCK, H), log_decay.reshape(blocks, BLOCK, H), segment.reshape(blocks, BLOCK), seg_before)
    initial = jnp.zeros((H, P_SIZE, N), jnp.float32)
    final_state, ssm_out = lax.scan(jax.checkpoint(block_step), initial, fields)
    ssm_out = ssm_out.reshape(length, H, P_SIZE)
    mixer_out = (ssm_out + skip_gain[:, None] * heads_full).reshape(length, DI)
    gated_out = mixer_out * jax.nn.silu(projected[:, :DI])
    scale_out = lax.rsqrt(lax.optimization_barrier(jnp.mean(gated_out * gated_out, axis=-1, keepdims=True)) + EPSILON)
    normed_out = low(gated_out * scale_out * gain_out)
    return inputs + jnp.dot(normed_out, weight_out, precision=HIGHEST)

def reference(block_input, out_cotangent, doc_lengths, norm_gain, in_weight, conv_weight, conv_bias, step_bias, decay_log, skip_gain, out_gain, out_weight):
    params = tuple((value.astype(jnp.float32) for value in (norm_gain, in_weight, conv_weight, conv_bias, step_bias, decay_log, skip_gain, out_gain, out_weight)))
    length = block_input.shape[1]

    def per_sequence(running, fields):
        inputs, cotangent, lengths_row = fields
        segment = segments_of(lengths_row, length)

        def forward(weights_all, values):
            return block(weights_all, values, segment)
        outcome, pullback = jax.vjp(forward, params, inputs.astype(jnp.float32))
        grad_params, grad_inputs = pullback(cotangent.astype(jnp.float32))
        running = jax.tree.map(lambda left, right: left + right, running, grad_params)
        return (running, (outcome.astype(jnp.bfloat16), grad_inputs.astype(jnp.bfloat16)))
    zero_grads = jax.tree.map(jnp.zeros_like, params)
    totals, (outputs, input_grads) = lax.scan(per_sequence, zero_grads, (block_input, out_cotangent, doc_lengths))
    return (outputs, input_grads, totals[0], totals[1], totals[2], totals[3], totals[4], totals[5], totals[6], totals[7], totals[8])
```

```python
import functools

import jax
import jax.numpy as jnp
from jax import lax
from jax.experimental import pallas as pl
from jax.experimental.pallas import tpu as pltpu
from jax.sharding import PartitionSpec as P

H = 24
PS = 64
N = 128
KCONV = 4
BLOCK = 256
DI = 1536
CONVCH = 1792
EPS = 1e-05
BF = jnp.bfloat16
F32 = jnp.float32
ANY = pl.ANY
VMEM_LIMIT = 56 * 1024 * 1024


def dot(a, b):
    return lax.dot_general(a, b, (((1,), (0,)), ((), ())), preferred_element_type=F32)


def dot_nt(a, b):
    return lax.dot_general(a, b, (((1,), (1,)), ((), ())), preferred_element_type=F32)


def dot_tn(a, b):
    return lax.dot_general(a, b, (((0,), (0,)), ((), ())), preferred_element_type=F32)


def pieces(value, count):
    out = []
    for _ in range(count):
        part = value.astype(BF)
        out.append(part)
        value = value - part.astype(F32)
    return out


def sigmoid(value):
    return 0.5 * jnp.tanh(0.5 * value) + 0.5


def iota(shape, dim):
    return lax.broadcasted_iota(jnp.int32, shape, dim)


def segments(bounds, position):
    seg = functools.reduce(
        lambda total, bound: total + jnp.where(position >= bound, 1, 0),
        bounds,
        jnp.zeros_like(position),
    )
    return jnp.where(position < 0, -1, seg)


def expand(table, pairs):
    low = iota((table.shape[0], 128), 1) < PS
    return jnp.concatenate(
        [
            jnp.where(low, table[:, 2 * p : 2 * p + 1], table[:, 2 * p + 1 : 2 * p + 2])
            for p in range(pairs)
        ],
        axis=1,
    )


def head_select(lanes):
    return (iota((lanes, 128), 0) // PS == iota((lanes, 128), 1)).astype(BF)


def head_sum(value):
    select = head_select(value.shape[1])
    return sum(dot(part, select) for part in pieces(value, 2))


def head_rows(row, lanes):
    mine = iota((lanes, 128), 0) // PS == iota((lanes, 128), 1)
    return jnp.sum(jnp.where(mine, row, 0.0), axis=1, keepdims=True)


def load_blocks(refs, dest, me, rows, sem):
    copies = [
        pltpu.make_async_copy(
            ref, dest.at[pl.ds(pl.multiple_of((me ^ k) * rows, 16), rows)], sem.at[k]
        )
        for k, ref in enumerate(refs)
    ]
    for copy in copies:
        copy.start()
    return copies


def conv_forward(cext, taps, bounds, start, width):
    col = start + iota((BLOCK, 1), 0)
    seg = segments(bounds, col)
    masks, pre = [], taps[KCONV : KCONV + 1, :]
    for k in range(KCONV):
        back = KCONV - 1 - k
        same = jnp.where(segments(bounds, col - back) == seg, 1.0, 0.0)
        masks.append(same)
        pre = pre + taps[k : k + 1, :] * (cext[pl.ds(8 - back, BLOCK), :] * same)
    return pre, masks


def scan_terms(raw, heads, bounds, start):
    z = raw + heads[0:1, :]
    step = jnp.maximum(z, 0.0) + jnp.log1p(jnp.exp(-jnp.abs(z)))
    rate = -jnp.exp(heads[1:2, :])
    log_decay = step * rate
    tri = (iota((BLOCK, BLOCK), 0) >= iota((BLOCK, BLOCK), 1)).astype(BF)
    cum = sum(dot(tri, part) for part in pieces(log_decay, 3))
    col = segments(bounds, start + iota((BLOCK, 1), 0))
    row = segments(bounds, start + iota((1, BLOCK), 1))
    before = segments(bounds, start - 1)
    last = segments(bounds, start + BLOCK - 1)
    below = iota((BLOCK, BLOCK), 0) >= iota((BLOCK, BLOCK), 1)
    bias = jnp.where(below, jnp.where(col == row, 0.0, -1e30), -1e30)
    tail = cum[BLOCK - 1 : BLOCK, :]
    enter = jnp.where(col == before, jnp.exp(cum), 0.0)
    end = jnp.where(col == last, jnp.exp(tail - cum), 0.0)
    keep = jnp.where(last == before, jnp.exp(tail), 0.0)
    return z, step, rate, cum, bias, enter, end, keep


def forward_kernel(n, heads, scal, *refs):
    xs, ws = refs[:n], refs[n : 2 * n]
    gain, taps, hp, skip = refs[2 * n : 2 * n + 4]
    normed_o, conv_o, raw_o, mixer_o, start_o = refs[2 * n + 4 : 2 * n + 9]
    xv, wv, cext, state, sem_x, sem_w = refs[2 * n + 9 :]
    lanes = heads * PS
    width = lanes + 2 * N
    b = pl.program_id(0)
    bounds = [scal[i] for i in range(2, scal.shape[0])]
    start = b * BLOCK

    @pl.when(b == 0)
    def _():
        me = scal[0]
        copies = load_blocks(xs, xv, me, BLOCK, sem_x)
        copies += load_blocks(ws, wv, me, ws[0].shape[0], sem_w)
        cext[0:8, :] = jnp.zeros((8, width), F32)
        state[...] = jnp.zeros_like(state)
        for copy in copies:
            copy.wait()

    x = xv[pl.ds(pl.multiple_of(start, BLOCK), BLOCK), :].astype(F32)
    scale = lax.rsqrt(jnp.mean(x * x, axis=1, keepdims=True) + EPS)
    normed = (x * scale * gain[...]).astype(BF)
    normed_o[...] = normed
    proj = dot(normed, wv[...]).astype(BF)
    conv_o[...] = proj[:, :width]
    raw = proj[:, width:].astype(F32)
    raw_o[...] = raw
    cext[8:, :] = proj[:, :width].astype(F32)
    pre, _ = conv_forward(cext, taps, bounds, start, width)
    cext[0:8, :] = cext[BLOCK:, :]
    act = pre * sigmoid(pre)
    low = act.astype(BF)
    full = act[:, :lanes]
    keys, query = low[:, lanes : lanes + N], low[:, lanes + N :]
    _, step, _, cum, bias, enter, end, keep = scan_terms(raw, hp, bounds, start)
    cum_t, step_t = cum.T, step.T
    gram = dot_nt(query, keys)
    start_state = state[...]
    start_o[0] = start_state
    inter = dot_nt(query, start_state.astype(BF)) * expand(enter, heads // 2)
    weighted = (full * expand(end * step, heads // 2)).astype(BF)
    state[...] = head_rows(keep, lanes) * start_state + dot_tn(weighted, keys)
    rest = inter + skip[...] * full
    first = iota((BLOCK, 2 * PS), 1) < PS
    for p in range(heads // 2):
        at = slice(2 * PS * p, 2 * PS * (p + 1))
        pair = low[:, at]
        halves = (jnp.where(first, pair, 0), jnp.where(first, 0, pair))
        for t in range(2):
            rows, cols = slice(128 * t, 128 * (t + 1)), slice(0, 128 * (t + 1))
            total = rest[rows, at]
            for i in range(2):
                h = 2 * p + i
                decay = jnp.exp(cum[rows, h : h + 1] - cum_t[h : h + 1, cols] + bias[rows, cols])
                weights = (gram[rows, cols] * decay * step_t[h : h + 1, cols]).astype(BF)
                total = total + dot(weights, halves[i][cols, :])
            mixer_o[rows, at] = total


def gate_kernel(n, scal, *refs):
    gs, ws = refs[:n], refs[n : 2 * n]
    normed, mixer, wo, gain = refs[2 * n : 2 * n + 4]
    raw_o, gno_o, stat_o = refs[2 * n + 4 : 2 * n + 7]
    gv, wv, sem_g, sem_w = refs[2 * n + 7 :]
    b = pl.program_id(0)

    @pl.when(b == 0)
    def _():
        me = scal[0]
        copies = load_blocks(gs, gv, me, BLOCK, sem_g)
        copies += load_blocks(ws, wv, me, ws[0].shape[0], sem_w)
        for copy in copies:
            copy.wait()

    raw = dot(normed[...], wv[...]).astype(BF)
    raw_o[...] = raw
    gate = raw.astype(F32)
    gated = mixer[...] * (gate * sigmoid(gate))
    g = gv[pl.ds(pl.multiple_of(b * BLOCK, BLOCK), BLOCK), :]
    gno = dot_nt(g, wo[...])
    gno_o[...] = gno
    first = jnp.sum(gated * gated, axis=1, keepdims=True)
    second = jnp.sum(gno * gain[...] * gated, axis=1, keepdims=True)
    lane = iota((BLOCK, 128), 1)
    both = jnp.where(lane == 0, first, jnp.where(lane == 1, second, 0.0))
    stat_o[...] = both.T[0:8, :]


def output_kernel(n, nd, inner, scal, *refs):
    gs = refs[:n]
    stats = refs[n : 2 * n]
    normed, mixer, raw, gno, wo, gain = refs[2 * n : 2 * n + 6]
    out_o, gssm_o, ggr_o, dwo_o, dwg_o = refs[2 * n + 6 : 2 * n + 11]
    gv, acc_o, acc_g, sem_g = refs[2 * n + 11 :]
    b = pl.program_id(0)

    @pl.when(b == 0)
    def _():
        copies = load_blocks(gs, gv, scal[0], BLOCK, sem_g)
        acc_o[...] = jnp.zeros_like(acc_o)
        acc_g[...] = jnp.zeros_like(acc_g)
        for copy in copies:
            copy.wait()

    stat = functools.reduce(lambda a, c: a + c, [s[...] for s in stats])
    stat = jnp.concatenate([stat, jnp.zeros((120, BLOCK), F32)], axis=0).T
    scale = lax.rsqrt(stat[:, 0:1] * (1.0 / inner) + EPS)
    mean = stat[:, 1:2] * (1.0 / inner)
    mix = mixer[...]
    gate = raw[...].astype(F32)
    sig = sigmoid(gate)
    act = gate * sig
    gated = mix * act
    normed_out = (gated * scale * gain[...]).astype(BF)
    g = gv[pl.ds(pl.multiple_of(b * BLOCK, BLOCK), BLOCK), :]
    out_o[0] = dot(normed_out, wo[...]).astype(BF)
    acc_o[...] += dot_tn(normed_out, g)
    grad_gated = scale * (gno[...] * gain[...] - gated * (mean * scale * scale))
    grad_raw = (grad_gated * mix * (sig * (1.0 + gate * (1.0 - sig)))).astype(BF)
    ggr_o[...] = grad_raw
    gssm_o[...] = (grad_gated * act).astype(BF)
    acc_g[...] += dot_tn(normed[...], grad_raw)

    @pl.when(b == pl.num_programs(0) - 1)
    def _():
        store_shares(acc_g, dwg_o, n, nd, scal)
        share = acc_o.shape[0] // nd
        for d in range(nd):
            dwo_o[d ^ scal[1] if nd > 1 else d] = acc_o[d * share : (d + 1) * share, :].astype(BF)


def store_shares(acc, out, n, nd, scal):
    rows = acc.shape[0] // n
    share = rows // nd
    for j in range(n):
        for d in range(nd):
            at = j * rows + d * share
            out[j ^ scal[0], d ^ scal[1] if nd > 1 else d] = acc[at : at + share, :].astype(BF)


def scan_kernel(n, nd, heads, scal, *refs):
    ws, wgs = refs[:n], refs[n : 2 * n]
    normed, conv, conv_before, raw, starts, gssm, ggr, taps, hp, skip = refs[2 * n : 2 * n + 10]
    gn_o, dw_o, small_o = refs[2 * n + 10 : 2 * n + 13]
    wv, wgv, cext, gext, end_grad, acc, ggram, ght, sem_w, sem_g = refs[2 * n + 13 :]
    lanes = heads * PS
    width = lanes + 2 * N
    i = pl.program_id(0)
    b = pl.num_programs(0) - 1 - i
    bounds = [scal[k] for k in range(2, scal.shape[0])]
    start = b * BLOCK
    pairs = heads // 2

    @pl.when(i == 0)
    def _():
        copies = load_blocks(ws, wv, scal[0], ws[0].shape[0], sem_w)
        copies += load_blocks(wgs, wgv, scal[0], wgs[0].shape[0], sem_g)
        gext[BLOCK:, :] = jnp.zeros((8, width), F32)
        end_grad[...] = jnp.zeros_like(end_grad)
        acc[...] = jnp.zeros_like(acc)
        small_o[...] = jnp.zeros_like(small_o)
        for copy in copies:
            copy.wait()

    halo = conv_before[8:16, :].astype(F32)
    cext[0:8, :] = jnp.where(b > 0, halo, 0.0)
    cext[8:, :] = conv[...].astype(F32)
    pre, masks = conv_forward(cext, taps, bounds, start, width)
    sig = sigmoid(pre)
    act = pre * sig
    low = act.astype(BF)
    full = act[:, :lanes]
    keys, query = low[:, lanes : lanes + N], low[:, lanes + N :]
    z, step, rate, cum, bias, enter, end, keep = scan_terms(raw[...], hp, bounds, start)
    cum_t, step_t, enter_t = cum.T, step.T, enter.T
    gram = dot_nt(query, keys)
    grad = gssm[...]
    grad_f = grad.astype(F32)
    grad_t = grad_f.T.astype(BF)
    first = iota((BLOCK, 2 * PS), 1) < PS
    lane = iota((128, 128), 1)
    row_totals = [jnp.zeros((128, 128), F32), jnp.zeros((128, 128), F32)]
    col_totals = []
    ggram[...] = jnp.zeros_like(ggram)
    for p in range(pairs):
        at = slice(2 * PS * p, 2 * PS * (p + 1))
        pair = low[:, at]
        halves = (jnp.where(first, pair, 0), jnp.where(first, 0, pair))
        for k in range(2):
            h = 2 * p + k
            own = slice(PS * h, PS * (h + 1))
            cols_total = None
            for t in range(2):
                rows, cols = slice(128 * t, 128 * (t + 1)), slice(0, 128 * (t + 1))
                decay = jnp.exp(cum[rows, h : h + 1] - cum_t[h : h + 1, cols] + bias[rows, cols])
                table = dot_nt(grad[rows, at], halves[k][cols, :])
                gram_here = gram[rows, cols]
                step_row = step_t[h : h + 1, cols]
                weights = (gram_here * decay * step_row).astype(BF)
                common = table * decay
                stepped = common * step_row
                ggram[rows, cols] += stepped
                col = jnp.sum(common * gram_here, axis=0, keepdims=True)
                total = jnp.sum(stepped * gram_here, axis=1, keepdims=True)
                row_totals[t] = jnp.where(lane == h, total, row_totals[t])
                part = dot(grad_t[own, rows], weights)
                if t == 0:
                    ght[own, 0:128] = part
                    cols_total = col
                else:
                    ght[own, 0:128] += part[:, 0:128]
                    ght[own, 128:256] = part[:, 128:256]
                    cols_total = col + jnp.concatenate(
                        [cols_total, jnp.zeros((1, 128), F32)], axis=1
                    )
            col_totals.append(cols_total)
    col_totals.append(jnp.zeros((128 - heads, BLOCK), F32))
    grad_step = jnp.concatenate(col_totals, axis=0).T
    grad_cum = jnp.concatenate(row_totals, axis=0) - step * grad_step
    gg = ggram[...].astype(BF)
    start_state = starts[0]
    start_low = start_state.astype(BF)
    grad_cum += head_sum(grad_f * dot_nt(query, start_low)) * enter
    entered = (grad_f * expand(enter, pairs)).astype(BF)
    grad_query = dot(gg, keys) + dot(entered, start_low)
    later = end_grad[...]
    end_low = later.astype(BF)
    scaled = end * step
    scaled_wide = expand(scaled, pairs)
    weighted = (full * scaled_wide).astype(BF)
    grad_weighted = dot_nt(keys, end_low)
    grad_keys = dot_tn(gg, query) + dot(weighted, end_low)
    grad_end = head_sum(grad_weighted * full)
    grad_step += grad_end * end
    end_terms = grad_end * scaled
    ones = jnp.ones((8, N), BF)
    held = sum(dot_nt(ones, part) for part in pieces(later * start_state, 2))
    grad_tail = jnp.sum(end_terms, axis=0, keepdims=True) + head_sum(held)[0:1, :] * keep
    final = iota((BLOCK, 1), 0) == BLOCK - 1
    grad_cum = grad_cum - end_terms + jnp.where(final, grad_tail, 0.0)
    upper = (iota((BLOCK, BLOCK), 0) <= iota((BLOCK, BLOCK), 1)).astype(BF)
    grad_log = sum(dot(upper, part) for part in pieces(grad_cum, 3))
    grad_step += grad_log * rate
    grad_rate = jnp.sum(grad_log * step, axis=0, keepdims=True)
    grad_heads = ght[...].T + grad_weighted * scaled_wide + grad_f * skip[...]
    grad_skip = jnp.sum(grad_f * full, axis=0, keepdims=True)
    grad_act = jnp.concatenate([grad_heads, grad_keys, grad_query], axis=1)
    grad_pre = grad_act * (sig * (1.0 + pre * (1.0 - sig)))
    gext[0:BLOCK, :] = grad_pre
    position = start + iota((BLOCK, 1), 0)
    seg = segments(bounds, position)
    grad_conv = jnp.zeros((BLOCK, width), F32)
    for k in range(KCONV):
        back = KCONV - 1 - k
        taken = cext[pl.ds(8 - back, BLOCK), :] * masks[k]
        small_o[k : k + 1, 0:width] += jnp.sum(grad_pre * taken, axis=0, keepdims=True)
        same = jnp.where(segments(bounds, position + back) == seg, 1.0, 0.0)
        grad_conv += taps[k : k + 1, :] * (gext[pl.ds(back, BLOCK), :] * same)
    small_o[4:5, 0:width] += jnp.sum(grad_pre, axis=0, keepdims=True)
    gext[BLOCK:, :] = gext[0:8, :]
    grad_raw = grad_step * sigmoid(z)
    small_o[0:1, width : width + 128] += jnp.sum(grad_raw, axis=0, keepdims=True)
    small_o[1:2, width : width + 128] += grad_rate * rate
    small_o[2:3, width : width + 128] += head_sum(jnp.broadcast_to(grad_skip, (8, lanes)))[0:1, :]
    here = normed[...]
    raw_low = grad_raw.astype(BF)
    small_o[:, width + 128 :] += dot_tn(raw_low, here)[0:8, :]
    conv_low = grad_conv.astype(BF)
    acc[...] += dot_tn(here, conv_low)
    gn = dot_nt(jnp.concatenate([conv_low, raw_low], axis=1), wv[...]) + dot_nt(ggr[...], wgv[...])
    gn_o[0] = gn.astype(BF)
    geared = jnp.concatenate(
        [grad_t[PS * h : PS * (h + 1), :].astype(F32) * enter_t[h : h + 1, :] for h in range(heads)],
        axis=0,
    ).astype(BF)
    end_grad[...] = head_rows(keep, lanes) * later + dot(geared, query)

    @pl.when(i == pl.num_programs(0) - 1)
    def _():
        store_shares(acc, dw_o, n, nd, scal)


def weights_kernel(n, own_heads, scal, gate, conv, step, weight, gain, out, gain_out):
    own = own_heads * PS
    me = scal[0]
    gate_v, conv_v = gate[0].astype(F32), conv[0].astype(F32)
    lanes = gate_v.shape[1] // n
    for q in range(n):

        @pl.when(me == q)
        def _(q=q):
            for k in range(n):
                at = (q ^ k) * own
                out[:, at : at + own] = gate_v[:, k * lanes : k * lanes + own]
                out[:, DI + at : DI + at + own] = conv_v[:, k * lanes : k * lanes + own]

    out[:, 2 * DI : 2 * DI + 2 * N] = conv_v[:, n * lanes :]
    out[:, 2 * DI + 2 * N :] = step[...]
    dots = jnp.sum(out[...] * weight[...].astype(F32), axis=1, keepdims=True)
    gain_out[...] = dots / gain[...]


def out_weight_kernel(scal, share, weight, gain, out, gain_out):
    value = share[0].astype(F32)
    out[...] = value
    gain_out[...] = jnp.sum(value * weight[...].astype(F32), axis=1, keepdims=True) / gain[...]


def xor(value, axis, k):
    return lax.ppermute(value, axis, [(s, s ^ k) for s in range(lax.axis_size(axis))])


def gather_xor(value, axis):
    out = [value]
    for k in range(1, lax.axis_size(axis)):
        out.append(xor(value, axis, k) if k % 2 == 0 or k == 1 else xor(out[k - 1], axis, 1))
    return out


def by_owner(parts, me):
    stacked = jnp.stack(parts)
    return [lax.dynamic_index_in_dim(stacked, me ^ j, 0, False) for j in range(len(parts))]


def stages(count):
    out, low = [], 0
    bits = count.bit_length() - 1
    while low < bits:
        take = 1 if low == 0 else min(2, bits - low)
        out.append((low, take))
        low += take
    return out


def scatter_dp(value, dim):
    total = value
    for low, take in stages(value.shape[dim]):
        radix = 1 << take
        shape = total.shape
        total = total.reshape(shape[:dim] + (shape[dim] // radix, radix) + shape[dim + 1 :])
        index = lambda m: (slice(None),) * (dim + 1) + (m,)
        recv = [xor(total[index(m)], "dp", m << low) for m in range(1, radix)]
        mine = total[index(0)].astype(F32)
        for r in recv:
            mine = mine + r.astype(F32)
        total = mine.astype(BF)
    return total.reshape(total.shape[:dim] + total.shape[dim + 1 :])


def gather_dp(value):
    count = lax.axis_size("dp")
    out = value[None]
    for low, take in reversed(stages(count)):
        out = jnp.concatenate([out] + [xor(out, "dp", m << low) for m in range(1, 1 << take)], 0)
    order = [0]
    for low, take in reversed(stages(count)):
        order = [o | (m << low) for m in range(1 << take) for o in order]
    return out, order


def call(kernel, name, grid, scal, in_specs, args, out_specs, out_shape, scratch, flops, bytes_):
    return pl.pallas_call(
        kernel,
        grid_spec=pltpu.PrefetchScalarGridSpec(
            num_scalar_prefetch=1,
            grid=grid,
            in_specs=in_specs,
            out_specs=out_specs,
            scratch_shapes=scratch,
        ),
        out_shape=out_shape,
        name=name,
        compiler_params=pltpu.CompilerParams(vmem_limit_bytes=VMEM_LIMIT),
        cost_estimate=pl.CostEstimate(flops=flops, bytes_accessed=bytes_, transcendentals=0),
    )(scal, *args)


def local(
    block_input,
    out_cotangent,
    doc_lengths,
    norm_gain,
    in_weight,
    conv_weight,
    conv_bias,
    step_bias,
    decay_log,
    skip_gain,
    out_gain,
    out_weight,
):
    n, ndp = lax.axis_size("fsdp"), lax.axis_size("dp")
    me, dpi = lax.axis_index("fsdp"), lax.axis_index("dp")
    _, toks, model = block_input.shape
    length = toks * n
    nb = length // BLOCK
    own_heads = H // n
    heads = own_heads + own_heads % 2
    own, lanes = own_heads * PS, heads * PS
    width = lanes + 2 * N
    rows = model // n
    share = rows // ndp
    nd = ndp if share % 8 == 0 else 1
    x_own, g_own = block_input[0], out_cotangent[0]
    bounds = jnp.cumsum(doc_lengths[0])[:-1].astype(jnp.int32)
    scal = jnp.concatenate([jnp.stack([me, dpi]).astype(jnp.int32), bounds])

    small = jnp.concatenate([norm_gain, conv_bias, conv_weight.reshape(-1)])
    small = jnp.pad(small, (0, -small.shape[0] % 1024)).reshape(-1, 128)
    xs = gather_xor(x_own, "fsdp")
    smalls = by_owner(
        [small] + [xor(small, "fsdp", k) for k in range(1, n)], me
    )
    flat = jnp.stack(smalls).reshape(n, -1)
    chans = CONVCH // n
    gain_full = flat[:, :rows].reshape(1, model).astype(F32)
    conv_full = jnp.concatenate(
        [
            flat[:, rows + chans : rows + chans * (1 + KCONV)]
            .reshape(n, KCONV, chans)
            .transpose(1, 0, 2)
            .reshape(KCONV, CONVCH),
            flat[:, rows : rows + chans].reshape(1, CONVCH),
        ],
        axis=0,
    ).astype(F32)
    conv_heads = lax.dynamic_slice_in_dim(conv_full, me * own, own, 1)
    taps = jnp.concatenate(
        [jnp.pad(conv_heads, ((0, 0), (0, lanes - own))), conv_full[:, DI:]], axis=1
    )
    taps = jnp.pad(taps, ((0, 3), (0, 0)))
    hp = jnp.stack([step_bias, decay_log]).astype(F32)
    hp = jnp.pad(hp, ((0, 6), (0, 128 - own_heads)))
    skip = jnp.pad(jnp.repeat(skip_gain.astype(F32), PS), (0, lanes - own)).reshape(1, lanes)

    def columns(first, size, padded):
        part = in_weight[:, first : first + n * size].reshape(rows, n, size).transpose(1, 0, 2)
        return jnp.pad(part, ((0, 0), (0, 0), (0, padded - size)))

    shared = jnp.broadcast_to(in_weight[None, :, 2 * DI : 2 * DI + 2 * N], (n, rows, 2 * N))
    conv_cols = jnp.concatenate(
        [columns(DI, own, lanes), shared, columns(2 * DI + 2 * N, own_heads, 128)], axis=2
    )
    gate_cols = columns(0, own, lanes)

    def exchange(stacked):
        mine = [lax.dynamic_index_in_dim(stacked, me ^ k, 0, False) for k in range(n)]
        return [mine[0]] + [xor(mine[k], "fsdp", k) for k in range(1, n)]

    ws = exchange(conv_cols)
    wgs = exchange(gate_cols)
    gs = gather_xor(g_own, "fsdp")

    any_spec = pl.BlockSpec(memory_space=ANY)

    def whole(*shape):
        return pl.BlockSpec(shape, lambda b, s: (0,) * len(shape))

    def tokens(cols):
        return pl.BlockSpec((BLOCK, cols), lambda b, s: (b, 0))

    shape = jax.ShapeDtypeStruct
    normed, conv_in, raw_step, mixer, starts = call(
        functools.partial(forward_kernel, n, heads),
        "forward",
        (nb,),
        scal,
        [any_spec] * (2 * n) + [whole(1, model), whole(8, width), whole(8, 128), whole(1, lanes)],
        (*xs, *ws, gain_full, taps, hp, skip),
        [
            tokens(model),
            tokens(width),
            tokens(128),
            tokens(lanes),
            pl.BlockSpec((1, lanes, N), lambda b, s: (b, 0, 0)),
        ],
        [
            shape((length, model), BF),
            shape((length, width), BF),
            shape((length, 128), F32),
            shape((length, lanes), F32),
            shape((nb, lanes, N), F32),
        ],
        [
            pltpu.VMEM((length, model), BF),
            pltpu.VMEM((model, width + 128), BF),
            pltpu.VMEM((8 + BLOCK, width), F32),
            pltpu.VMEM((lanes, N), F32),
            pltpu.SemaphoreType.DMA((n,)),
            pltpu.SemaphoreType.DMA((n,)),
        ],
        9 * 10**9,
        10**7,
    )

    out_w = jnp.pad(out_weight, ((0, lanes - own), (0, 0)))
    out_g = jnp.pad(out_gain.astype(F32), (0, lanes - own)).reshape(1, lanes)
    raw_gate, gno, stat = call(
        functools.partial(gate_kernel, n),
        "gate",
        (nb,),
        scal,
        [any_spec] * (2 * n)
        + [tokens(model), tokens(lanes), whole(lanes, model), whole(1, lanes)],
        (*gs, *wgs, normed, mixer, out_w, out_g),
        [tokens(lanes), tokens(lanes), pl.BlockSpec((8, BLOCK), lambda b, s: (0, b))],
        [
            shape((length, lanes), BF),
            shape((length, lanes), F32),
            shape((8, length), F32),
        ],
        [
            pltpu.VMEM((length, model), BF),
            pltpu.VMEM((model, lanes), BF),
            pltpu.SemaphoreType.DMA((n,)),
            pltpu.SemaphoreType.DMA((n,)),
        ],
        2 * 10**9,
        10**7,
    )
    stats = [stat] + [xor(stat, "fsdp", k) for k in range(1, n)]

    out_part, gssm, ggr, dwo, dwg = call(
        functools.partial(output_kernel, n, nd, DI),
        "output",
        (nb,),
        scal,
        [any_spec] * n
        + [pl.BlockSpec((8, BLOCK), lambda b, s: (0, b))] * n
        + [tokens(model), tokens(lanes), tokens(lanes), tokens(lanes)]
        + [whole(lanes, model), whole(1, lanes)],
        (*gs, *stats, normed, mixer, raw_gate, gno, out_w, out_g),
        [
            pl.BlockSpec((1, BLOCK, model), lambda b, s: (b ^ s[0], 0, 0)),
            tokens(lanes),
            tokens(lanes),
            whole(nd, lanes // nd, model),
            whole(n, nd, rows // nd, lanes),
        ],
        [
            shape((nb, BLOCK, model), BF),
            shape((length, lanes), BF),
            shape((length, lanes), BF),
            shape((nd, lanes // nd, model), BF),
            shape((n, nd, rows // nd, lanes), BF),
        ],
        [
            pltpu.VMEM((length, model), BF),
            pltpu.VMEM((lanes, model), F32),
            pltpu.VMEM((model, lanes), F32),
            pltpu.SemaphoreType.DMA((n,)),
        ],
        3 * 10**9,
        10**7,
    )

    def token_sum(parts):
        paired = parts.reshape(n // 2, 2, BLOCK, model)
        other = xor(paired[:, 1], "fsdp", 1)
        both = (paired[:, 0].astype(F32) + other.astype(F32)).astype(BF)
        total = both[0].astype(F32)
        for k in range(2, n, 2):
            total = total + xor(both[k // 2], "fsdp", k).astype(F32)
        return total

    def row_sum(shares):
        mine = scatter_dp(shares, 1) if nd > 1 else shares[:, 0]
        return [mine[0]] + [xor(mine[k], "fsdp", k) for k in range(1, n)]

    def spread(value):
        if nd == 1:
            return lax.psum(value.astype(BF), "dp")[None]
        out, order = gather_dp(value.astype(BF))
        return out

    order = gather_order(ndp) if nd > 1 else [0]

    gate_share = spread(jnp.concatenate(row_sum(dwg), axis=1))
    wo_share = spread(scatter_dp(dwo, 0) if nd > 1 else dwo[0])
    result = x_own.astype(F32) + token_sum(out_part)
    block_output = result.astype(BF)[None]

    back = lambda b: nb - 1 - b

    def tokens_back(cols):
        return pl.BlockSpec((BLOCK, cols), lambda b, s: (back(b), 0))

    gn_part, dw, small_grads = call(
        functools.partial(scan_kernel, n, nd, heads),
        "scan_back",
        (nb,),
        scal,
        [any_spec] * (2 * n)
        + [
            tokens_back(model),
            tokens_back(width),
            pl.BlockSpec((16, width), lambda b, s: (jnp.maximum(back(b) * (BLOCK // 16) - 1, 0), 0)),
            tokens_back(128),
            pl.BlockSpec((1, lanes, N), lambda b, s: (back(b), 0, 0)),
            tokens_back(lanes),
            tokens_back(lanes),
            whole(8, width),
            whole(8, 128),
            whole(1, lanes),
        ],
        (*ws, *wgs, normed, conv_in, conv_in, raw_step, starts, gssm, ggr, taps, hp, skip),
        [
            pl.BlockSpec((1, BLOCK, model), lambda b, s: (back(b) ^ s[0], 0, 0)),
            whole(n, nd, rows // nd, width),
            whole(8, width + 128 + model),
        ],
        [
            shape((nb, BLOCK, model), BF),
            shape((n, nd, rows // nd, width), BF),
            shape((8, width + 128 + model), F32),
        ],
        [
            pltpu.VMEM((model, width + 128), BF),
            pltpu.VMEM((model, lanes), BF),
            pltpu.VMEM((8 + BLOCK, width), F32),
            pltpu.VMEM((BLOCK + 8, width), F32),
            pltpu.VMEM((lanes, N), F32),
            pltpu.VMEM((model, width), F32),
            pltpu.VMEM((BLOCK, BLOCK), F32),
            pltpu.VMEM((lanes, BLOCK), F32),
            pltpu.SemaphoreType.DMA((n,)),
            pltpu.SemaphoreType.DMA((n,)),
        ],
        12 * 10**9,
        10**7,
    )

    conv_parts = row_sum(dw)
    shared_sum = conv_parts[0][:, lanes:].astype(F32)
    for part in conv_parts[1:]:
        shared_sum = shared_sum + part[:, lanes:].astype(F32)
    conv_share = spread(
        jnp.concatenate([part[:, :lanes] for part in conv_parts] + [shared_sum.astype(BF)], axis=1)
    )

    total_in = token_sum(gn_part)
    inputs = x_own.astype(F32)
    scale_in = lax.rsqrt(jnp.mean(inputs * inputs, axis=-1, keepdims=True) + EPS)
    gained = total_in * gain_full
    input_grad = scale_in * (
        gained - inputs * jnp.mean(gained * inputs, axis=-1, keepdims=True) * scale_in * scale_in
    ) + g_own.astype(F32)
    input_grad = input_grad.astype(BF)[None]

    if nd > 1:
        for low, take in stages(ndp):
            small_grads = small_grads + sum(
                xor(small_grads, "dp", m << low) for m in range(1, 1 << take)
            )
    else:
        small_grads = lax.psum(small_grads, "dp")
    parts = [small_grads] + [xor(small_grads, "fsdp", k) for k in range(1, n)]
    ordered = by_owner(parts, me)
    conv_grads = jnp.concatenate(
        [part[:5, :own] for part in ordered] + [sum(part[:5, lanes:width] for part in parts)], axis=1
    )
    conv_grads = lax.dynamic_slice_in_dim(conv_grads, me * chans, chans, 1)
    head_grads = small_grads[:3, width : width + own_heads]
    step_rows = jnp.concatenate([part[:own_heads, width + 128 :] for part in ordered], axis=0)
    step_cols = lax.dynamic_slice_in_dim(step_rows, me * rows, rows, 1).T

    def place(e, s):
        return functools.reduce(lambda a, c: jnp.where(e == c[0], c[1], a), list(enumerate(order)), 0) ^ (
            s[1] if nd > 1 else 0
        )

    part_rows = rows // nd
    grad_in, grad_gain = call(
        functools.partial(weights_kernel, n, own_heads),
        "in_weight_grad",
        (nd,),
        scal,
        [
            pl.BlockSpec((1, part_rows, n * lanes), lambda e, s: (e, 0, 0)),
            pl.BlockSpec((1, part_rows, n * lanes + 2 * N), lambda e, s: (e, 0, 0)),
            pl.BlockSpec((part_rows, H), lambda e, s: (place(e, s), 0)),
            pl.BlockSpec((part_rows, in_weight.shape[1]), lambda e, s: (place(e, s), 0)),
            pl.BlockSpec((part_rows, 1), lambda e, s: (place(e, s), 0)),
        ],
        (gate_share, conv_share, step_cols, in_weight, norm_gain.astype(F32).reshape(rows, 1)),
        [
            pl.BlockSpec((part_rows, in_weight.shape[1]), lambda e, s: (place(e, s), 0)),
            pl.BlockSpec((part_rows, 1), lambda e, s: (place(e, s), 0)),
        ],
        [shape(in_weight.shape, F32), shape((rows, 1), F32)],
        [],
        10**6,
        6 * 10**6,
    )
    own_rows = lanes // nd
    grad_out, grad_out_gain = call(
        out_weight_kernel,
        "out_weight_grad",
        (nd,),
        scal,
        [
            pl.BlockSpec((1, own_rows, model), lambda e, s: (e, 0, 0)),
            pl.BlockSpec((own_rows, model), lambda e, s: (place(e, s), 0)),
            pl.BlockSpec((own_rows, 1), lambda e, s: (place(e, s), 0)),
        ],
        (wo_share, out_w, jnp.pad(out_gain.astype(F32), (0, lanes - own), constant_values=1.0).reshape(lanes, 1)),
        [
            pl.BlockSpec((own_rows, model), lambda e, s: (place(e, s), 0)),
            pl.BlockSpec((own_rows, 1), lambda e, s: (place(e, s), 0)),
        ],
        [shape((lanes, model), F32), shape((lanes, 1), F32)],
        [],
        10**6,
        3 * 10**6,
    )
    return (
        block_output,
        input_grad,
        grad_gain.reshape(rows),
        grad_in,
        conv_grads[:KCONV],
        conv_grads[KCONV],
        head_grads[0],
        head_grads[1],
        head_grads[2],
        grad_out_gain[:own].reshape(own),
        grad_out[:own],
    )


def gather_order(count):
    order = [0]
    for low, take in reversed(stages(count)):
        order = [o | (m << low) for m in range(1 << take) for o in order]
    return order


def solution(mesh):
    return jax.shard_map(
        local,
        mesh=mesh,
        in_specs=(
            P("dp", "fsdp", None),
            P("dp", "fsdp", None),
            P("dp", None),
            P("fsdp"),
            P("fsdp", None),
            P(None, "fsdp"),
            P("fsdp"),
            P("fsdp"),
            P("fsdp"),
            P("fsdp"),
            P("fsdp"),
            P("fsdp", None),
        ),
        out_specs=(
            P("dp", "fsdp", None),
            P("dp", "fsdp", None),
            P("fsdp"),
            P("fsdp", None),
            P(None, "fsdp"),
            P("fsdp"),
            P("fsdp"),
            P("fsdp"),
            P("fsdp"),
            P("fsdp"),
            P("fsdp", None),
        ),
        check_vma=False,
    )
```

```python
import functools

import jax
import jax.numpy as jnp
from jax import lax
from jax.experimental import pallas as pl
from jax.experimental.pallas import tpu as pltpu
from jax.sharding import PartitionSpec as P

H = 24
PS = 64
N = 128
KCONV = 4
BLOCK = 256
DI = 1536
CONVCH = 1792
EPS = 1e-05
BF = jnp.bfloat16
F32 = jnp.float32
ANY = pltpu.HBM
VMEM_LIMIT = 24 * 1024 * 1024


def dot(a, b):
    return lax.dot_general(a, b, (((1,), (0,)), ((), ())), preferred_element_type=F32)


def dot_nt(a, b):
    return lax.dot_general(a, b, (((1,), (1,)), ((), ())), preferred_element_type=F32)


def dot_tn(a, b):
    return lax.dot_general(a, b, (((0,), (0,)), ((), ())), preferred_element_type=F32)


def pieces(value, count):
    out = []
    for _ in range(count):
        part = value.astype(BF)
        out.append(part)
        value = value - part.astype(F32)
    return out


def sigmoid(value):
    return 0.5 * jnp.tanh(0.5 * value) + 0.5


def iota(shape, dim):
    return lax.broadcasted_iota(jnp.int32, shape, dim)


def document_start(bounds, position):
    return functools.reduce(
        lambda start, bound: jnp.where(position >= bound, bound, start),
        bounds,
        jnp.zeros_like(position),
    )


def document_end(bounds, position):
    return functools.reduce(
        lambda end, bound: jnp.where(position < bound, bound, end),
        reversed(bounds),
        jnp.full_like(position, 1 << 30),
    )


def expand(table, pairs):
    low = iota((table.shape[0], 128), 1) < PS
    return jnp.concatenate(
        [
            jnp.where(low, table[:, 2 * p : 2 * p + 1], table[:, 2 * p + 1 : 2 * p + 2])
            for p in range(pairs)
        ],
        axis=1,
    )


def head_select(lanes):
    return (iota((lanes, 128), 0) // PS == iota((lanes, 128), 1)).astype(BF)


def head_sum(value):
    select = head_select(value.shape[1])
    return sum(dot(part, select) for part in pieces(value, 2))


def head_rows(row, lanes):
    mine = iota((lanes, 128), 0) // PS == iota((lanes, 128), 1)
    return jnp.sum(jnp.where(mine, row, 0.0), axis=1, keepdims=True)


def load_blocks(refs, dest, me, rows, sem, col=None):
    copies = []
    for k, ref in enumerate(refs):
        at = pl.ds(pl.multiple_of((me ^ k) * rows, 16), rows)
        to = dest.at[at] if col is None else dest.at[at, pl.ds(col[0], col[2])]
        ref = ref if col is None else ref.at[:, pl.ds(col[1], col[2])]
        copies.append(pltpu.make_async_copy(ref, to, sem.at[k]))
    for copy in copies:
        copy.start()
    return copies


def wait_block(ref, dest, me, b, sem):
    at = pl.ds(pl.multiple_of(b * BLOCK, BLOCK), BLOCK)
    pltpu.make_async_copy(ref, dest.at[at], sem.at[b ^ me]).wait()
    return dest[at, :]


def conv_forward(cext, taps, bounds, start):
    position = start + iota((BLOCK, 1), 0)
    depth = position - document_start(bounds, position)
    masks, pre = [], taps[KCONV : KCONV + 1, :]
    for k in range(KCONV):
        back = KCONV - 1 - k
        taken = cext[pl.ds(8 - back, BLOCK), :]
        if back:
            masks.append(jnp.where(depth >= back, 1.0, 0.0))
            taken = taken * masks[-1]
        pre = pre + taps[k : k + 1, :] * taken
    return pre, masks + [None]


def scan_terms(raw, heads, bounds, start):
    z = raw + heads[0:1, :]
    step = jnp.maximum(z, 0.0) + jnp.log1p(jnp.exp(-jnp.abs(z)))
    rate = -jnp.exp(heads[1:2, :])
    log_decay = step * rate
    tri = (iota((BLOCK, BLOCK), 0) >= iota((BLOCK, BLOCK), 1)).astype(BF)
    cum = sum(dot(tri, part) for part in pieces(log_decay, 3))
    position = start + iota((BLOCK, 1), 0)
    first = document_start(bounds, position)
    last_first = document_start(bounds, start + BLOCK - 1)
    other = start + iota((BLOCK, BLOCK), 1)
    bias = jnp.where((other <= position) & (other >= first), 0.0, -1e30)
    tail = cum[BLOCK - 1 : BLOCK, :]
    enter = jnp.where(first < start, jnp.exp(cum), 0.0)
    end = jnp.where(position >= last_first, jnp.exp(tail - cum), 0.0)
    keep = jnp.where(last_first < start, jnp.exp(tail), 0.0)
    return z, step, rate, cum, bias, enter, end, keep


def forward_kernel(n, heads, own_heads, scal, *refs):
    xs, ws, wks = refs[:n], refs[n : 2 * n], refs[2 * n : 3 * n]
    gain, taps, hp, skip = refs[3 * n : 3 * n + 4]
    normed_o, normed_t_o, conv_o, convk_o, raw_o, mixer_o, start_o = refs[3 * n + 4 : 3 * n + 11]
    xv, wv, cext, state, sem_x, sem_w, sem_k = refs[3 * n + 11 :]
    lanes = heads * PS
    width = lanes + 2 * N
    b = pl.program_id(0)
    bounds = [scal[i] for i in range(2, scal.shape[0])]
    start = b * BLOCK

    @pl.when(b == 0)
    def _():
        me = scal[0]
        load_blocks(xs, xv, me, BLOCK, sem_x)
        copies = load_blocks(ws, wv, me, ws[0].shape[0], sem_w, (0, 0, lanes))
        copies += load_blocks(wks, wv, me, ws[0].shape[0], sem_k, (lanes, 0, 2 * N + 128))
        cext[0:8, :] = jnp.zeros((8, width), F32)
        state[...] = jnp.zeros_like(state)
        for copy in copies:
            copy.wait()

    x = wait_block(xs[0], xv, scal[0], b, sem_x).astype(F32)
    scale = lax.rsqrt(jnp.mean(x * x, axis=1, keepdims=True) + EPS)
    normed = (x * scale * gain[...]).astype(BF)
    normed_o[...] = normed
    normed_t_o[...] = normed.T
    proj = dot(normed, wv[...]).astype(BF)
    conv_o[...] = proj[:, :lanes]
    convk_o[...] = proj[:, lanes:width]
    raw = pltpu.roll(proj[:, width:].astype(F32), 128 - scal[0] * own_heads, 1)
    raw_o[...] = raw
    cext[8:, :] = proj[:, :width].astype(F32)
    pre, _ = conv_forward(cext, taps, bounds, start)
    cext[0:8, :] = cext[BLOCK:, :]
    act = pre * sigmoid(pre)
    low = act.astype(BF)
    full = act[:, :lanes]
    keys, query = low[:, lanes : lanes + N], low[:, lanes + N :]
    _, step, _, cum, bias, enter, end, keep = scan_terms(raw, hp, bounds, start)
    cum_t, step_t = cum.T, step.T
    gram = dot_nt(query, keys)
    start_state = state[...]
    start_o[0] = start_state
    inter = dot_nt(query, start_state.astype(BF)) * expand(enter, heads // 2)
    weighted = (full * expand(end * step, heads // 2)).astype(BF)
    state[...] = head_rows(keep, lanes) * start_state + dot_tn(weighted, keys)
    rest = inter + skip[...] * full
    first = iota((BLOCK, 2 * PS), 1) < PS
    for p in range(heads // 2):
        at = slice(2 * PS * p, 2 * PS * (p + 1))
        pair = low[:, at]
        halves = (jnp.where(first, pair, 0), jnp.where(first, 0, pair))
        for t in range(2):
            rows, cols = slice(128 * t, 128 * (t + 1)), slice(0, 128 * (t + 1))
            total = rest[rows, at]
            for i in range(2):
                h = 2 * p + i
                decay = jnp.exp(cum[rows, h : h + 1] - cum_t[h : h + 1, cols] + bias[rows, cols])
                weights = (gram[rows, cols] * decay * step_t[h : h + 1, cols]).astype(BF)
                total = total + dot(weights, halves[i][cols, :])
            mixer_o[rows, at] = total


def gate_kernel(n, scal, *refs):
    gs, ws = refs[:n], refs[n : 2 * n]
    normed, mixer, wo, gain = refs[2 * n : 2 * n + 4]
    raw_o, gno_o, stat_o = refs[2 * n + 4 : 2 * n + 7]
    gv, wv, sem_g, sem_w = refs[2 * n + 7 :]
    b = pl.program_id(0)

    @pl.when(b == 0)
    def _():
        me = scal[0]
        load_blocks(gs, gv, me, BLOCK, sem_g)
        lanes = wv.shape[1]
        for copy in load_blocks(ws, wv, me, ws[0].shape[0], sem_w, (0, lanes, lanes)):
            copy.wait()

    raw = dot(normed[...], wv[...]).astype(BF)
    raw_o[...] = raw
    gate = raw.astype(F32)
    gated = mixer[...] * (gate * sigmoid(gate))
    g = wait_block(gs[0], gv, scal[0], b, sem_g)
    gno = dot_nt(g, wo[...])
    gno_o[...] = gno
    first = jnp.sum(gated * gated, axis=1, keepdims=True)
    second = jnp.sum(gno * gain[...] * gated, axis=1, keepdims=True)
    lane = iota((BLOCK, 128), 1)
    both = jnp.where(lane == 0, first, jnp.where(lane == 1, second, 0.0))
    stat_o[...] = both.T[0:8, :]


def output_kernel(n, nd, inner, scal, *refs):
    gs = refs[:n]
    stats = refs[n : 2 * n]
    normed_t, mixer, raw, gno, wo, gain = refs[2 * n : 2 * n + 6]
    out_o, gssm_o, ggr_o, early_o = refs[2 * n + 6 : 2 * n + 10]
    gv, acc_o, acc_g, sem_g = refs[2 * n + 10 :]
    b = pl.program_id(0)

    @pl.when(b == 0)
    def _():
        load_blocks(gs, gv, scal[0], BLOCK, sem_g)
        acc_o[...] = jnp.zeros_like(acc_o)
        acc_g[...] = jnp.zeros_like(acc_g)

    stat = functools.reduce(lambda a, c: a + c, [s[...] for s in stats])
    stat = jnp.concatenate([stat, jnp.zeros((120, BLOCK), F32)], axis=0).T
    scale = lax.rsqrt(stat[:, 0:1] * (1.0 / inner) + EPS)
    mean = stat[:, 1:2] * (1.0 / inner)
    mix = mixer[...]
    gate = raw[...].astype(F32)
    sig = sigmoid(gate)
    act = gate * sig
    gated = mix * act
    normed_out = (gated * scale * gain[...]).astype(BF)
    g = wait_block(gs[0], gv, scal[0], b, sem_g)
    out_o[0] = dot(normed_out, wo[...]).astype(BF)
    acc_o[...] += dot_tn(normed_out, g)
    grad_gated = scale * (gno[...] * gain[...] - gated * (mean * scale * scale))
    grad_raw = (grad_gated * mix * (sig * (1.0 + gate * (1.0 - sig)))).astype(BF)
    ggr_o[...] = grad_raw
    gssm_o[...] = (grad_gated * act).astype(BF)
    acc_g[...] += dot(normed_t[...], grad_raw)

    @pl.when(b == pl.num_programs(0) - 1)
    def _():
        share, lanes, model = acc_o.shape[0] // nd, acc_g.shape[1], acc_o.shape[1]
        rows = model // n
        part, side = rows // nd, max(1, model // lanes)
        for d in range(nd):
            to = d ^ scal[1] if nd > 1 else d
            early_o[to, 0:share, :] = acc_o[d * share : (d + 1) * share, :].astype(BF)
            for j in range(n):
                k = j ^ scal[0]
                first = pl.multiple_of(share + k // side * part, 8)
                value = acc_g[j * rows + d * part : j * rows + (d + 1) * part, :].astype(BF)
                for c in range(side):

                    @pl.when(k % side == c)
                    def _(c=c, value=value, first=first, to=to):
                        early_o[to, pl.ds(first, part), c * lanes : (c + 1) * lanes] = value


def store_shares(acc, out, n, nd, scal):
    rows = acc.shape[0] // n
    share = rows // nd
    for j in range(n):
        for d in range(nd):
            at = j * rows + d * share
            out[j ^ scal[0], d ^ scal[1] if nd > 1 else d] = acc[at : at + share, :].astype(BF)


def scan_kernel(n, nd, heads, own_heads, scal, *refs):
    normed_t, conv, conv_before, convk, convk_before, raw, starts, gssm, taps, hp, skip = refs[:11]
    proj_o, dw_o, small_o = refs[11:14]
    cext, gext, end_grad, acc, ggram, ght = refs[14:]
    lanes = heads * PS
    width = lanes + 2 * N
    i = pl.program_id(0)
    b = pl.num_programs(0) - 1 - i
    bounds = [scal[k] for k in range(2, scal.shape[0])]
    start = b * BLOCK
    pairs = heads // 2

    @pl.when(i == 0)
    def _():
        gext[BLOCK:, :] = jnp.zeros((8, width), F32)
        end_grad[...] = jnp.zeros_like(end_grad)
        acc[...] = jnp.zeros_like(acc)
        small_o[...] = jnp.zeros_like(small_o)

    for source, halo, at in ((conv, conv_before, slice(0, lanes)), (convk, convk_before, slice(lanes, width))):
        cext[0:8, at] = jnp.where(b > 0, halo[8:16, :].astype(F32), 0.0)
        cext[8:, at] = source[...].astype(F32)
    pre, masks = conv_forward(cext, taps, bounds, start)
    sig = sigmoid(pre)
    act = pre * sig
    low = act.astype(BF)
    full = act[:, :lanes]
    keys, query = low[:, lanes : lanes + N], low[:, lanes + N :]
    z, step, rate, cum, bias, enter, end, keep = scan_terms(raw[...], hp, bounds, start)
    cum_t, step_t, enter_t = cum.T, step.T, enter.T
    gram = dot_nt(query, keys)
    grad = gssm[...]
    grad_f = grad.astype(F32)
    grad_t = grad_f.T.astype(BF)
    first = iota((BLOCK, 2 * PS), 1) < PS
    lane = iota((128, 128), 1)
    row_totals = [jnp.zeros((128, 128), F32), jnp.zeros((128, 128), F32)]
    col_totals = []
    ggram[...] = jnp.zeros_like(ggram)
    for p in range(pairs):
        at = slice(2 * PS * p, 2 * PS * (p + 1))
        pair = low[:, at]
        halves = (jnp.where(first, pair, 0), jnp.where(first, 0, pair))
        for k in range(2):
            h = 2 * p + k
            own = slice(PS * h, PS * (h + 1))
            cols_total = None
            for t in range(2):
                rows, cols = slice(128 * t, 128 * (t + 1)), slice(0, 128 * (t + 1))
                decay = jnp.exp(cum[rows, h : h + 1] - cum_t[h : h + 1, cols] + bias[rows, cols])
                table = dot_nt(grad[rows, at], halves[k][cols, :])
                gram_here = gram[rows, cols]
                step_row = step_t[h : h + 1, cols]
                weights = (gram_here * decay * step_row).astype(BF)
                common = table * decay
                stepped = common * step_row
                ggram[rows, cols] += stepped
                col = jnp.sum(common * gram_here, axis=0, keepdims=True)
                total = jnp.sum(stepped * gram_here, axis=1, keepdims=True)
                row_totals[t] = jnp.where(lane == h, total, row_totals[t])
                part = dot(grad_t[own, rows], weights)
                if t == 0:
                    ght[own, 0:128] = part
                    cols_total = col
                else:
                    ght[own, 0:128] += part[:, 0:128]
                    ght[own, 128:256] = part[:, 128:256]
                    cols_total = col + jnp.concatenate(
                        [cols_total, jnp.zeros((1, 128), F32)], axis=1
                    )
            col_totals.append(cols_total)
    col_totals.append(jnp.zeros((128 - heads, BLOCK), F32))
    grad_step = jnp.concatenate(col_totals, axis=0).T
    grad_cum = jnp.concatenate(row_totals, axis=0) - step * grad_step
    gg = ggram[...].astype(BF)
    start_state = starts[0]
    start_low = start_state.astype(BF)
    grad_cum += head_sum(grad_f * dot_nt(query, start_low)) * enter
    entered = (grad_f * expand(enter, pairs)).astype(BF)
    grad_query = dot(gg, keys) + dot(entered, start_low)
    later = end_grad[...]
    end_low = later.astype(BF)
    scaled = end * step
    scaled_wide = expand(scaled, pairs)
    weighted = (full * scaled_wide).astype(BF)
    grad_weighted = dot_nt(keys, end_low)
    grad_keys = dot_tn(gg, query) + dot(weighted, end_low)
    grad_end = head_sum(grad_weighted * full)
    grad_step += grad_end * end
    end_terms = grad_end * scaled
    ones = jnp.ones((8, N), BF)
    held = sum(dot_nt(ones, part) for part in pieces(later * start_state, 2))
    grad_tail = jnp.sum(end_terms, axis=0, keepdims=True) + head_sum(held)[0:1, :] * keep
    final = iota((BLOCK, 1), 0) == BLOCK - 1
    grad_cum = grad_cum - end_terms + jnp.where(final, grad_tail, 0.0)
    upper = (iota((BLOCK, BLOCK), 0) <= iota((BLOCK, BLOCK), 1)).astype(BF)
    grad_log = sum(dot(upper, part) for part in pieces(grad_cum, 3))
    grad_step += grad_log * rate
    grad_rate = jnp.sum(grad_log * step, axis=0, keepdims=True)
    grad_heads = ght[...].T + grad_weighted * scaled_wide + grad_f * skip[...]
    grad_skip = jnp.sum(grad_f * full, axis=0, keepdims=True)
    grad_act = jnp.concatenate([grad_heads, grad_keys, grad_query], axis=1)
    grad_pre = grad_act * (sig * (1.0 + pre * (1.0 - sig)))
    conv_low = conv_backward(grad_pre, gext, cext, masks, taps, bounds, start, small_o).astype(BF)
    grad_raw = grad_step * sigmoid(z)
    small_o[0:1, width : width + 128] += jnp.sum(grad_raw, axis=0, keepdims=True)
    small_o[1:2, width : width + 128] += grad_rate * rate
    small_o[2:3, width : width + 128] += head_sum(jnp.broadcast_to(grad_skip, (8, lanes)))[0:1, :]
    here = normed_t[...]
    raw_low = grad_raw.astype(BF)
    small_o[:, width + 128 :] += dot_nt(raw_low.T[0:16, :], here)[0:8, :]
    acc[...] += dot(here, conv_low)
    proj_o[:, :width] = conv_low
    proj_o[:, width:] = pltpu.roll(grad_raw, scal[0] * own_heads, 1).astype(BF)
    geared = jnp.concatenate(
        [grad_t[PS * h : PS * (h + 1), :].astype(F32) * enter_t[h : h + 1, :] for h in range(heads)],
        axis=0,
    ).astype(BF)
    end_grad[...] = head_rows(keep, lanes) * later + dot(geared, query)

    @pl.when(i == pl.num_programs(0) - 1)
    def _():
        store_shares(acc, dw_o, n, nd, scal)


def conv_backward(grad_pre, gext, cext, masks, taps, bounds, start, small_o):
    count = grad_pre.shape[1]
    gext[0:BLOCK, :] = grad_pre
    position = start + iota((BLOCK, 1), 0)
    left = document_end(bounds, position) - position
    total = None
    for k in range(KCONV):
        back = KCONV - 1 - k
        taken = cext[pl.ds(8 - back, BLOCK), :]
        after = gext[pl.ds(back, BLOCK), :]
        if back:
            taken = taken * masks[k]
            after = after * jnp.where(left > back, 1.0, 0.0)
        small_o[k : k + 1, 0:count] += jnp.sum(grad_pre * taken, axis=0, keepdims=True)
        term = taps[k : k + 1, :] * after
        total = term if total is None else total + term
    small_o[4:5, 0:count] += jnp.sum(grad_pre, axis=0, keepdims=True)
    gext[BLOCK:, :] = gext[0:8, :]
    return total


def normed_kernel(n, lanes, scal, *refs):
    ws, wks = refs[:n], refs[n : 2 * n]
    proj, ggr, gn_o, wv, wgv, sem_w, sem_k, sem_g = refs[2 * n :]

    @pl.when(pl.program_id(0) == 0)
    def _():
        rows = ws[0].shape[0]
        copies = load_blocks(ws, wv, scal[0], rows, sem_w, (0, 0, lanes))
        copies += load_blocks(wks, wv, scal[0], rows, sem_k, (lanes, 0, 2 * N + 128))
        copies += load_blocks(ws, wgv, scal[0], rows, sem_g, (0, lanes, lanes))
        for copy in copies:
            copy.wait()

    gn_o[0] = (dot_nt(proj[...], wv[...]) + dot_nt(ggr[...], wgv[...])).astype(BF)


def rows_dot(value, weight):
    product = value * weight.astype(F32)
    ones = jnp.ones((8, product.shape[1]), BF)
    return sum(dot_nt(ones, part) for part in pieces(product, 2))


def weights_kernel(n, own, order, scal, *refs):
    late, step, weight, gain, out, gain_o = refs
    rows, lanes = late.shape[1], (late.shape[2] - 2 * N) // (2 * n)
    me = scal[0]
    at = [
        0 if len(order) == 1 else pl.multiple_of((place ^ scal[1]) * rows, 8) for place in order
    ]

    def put(first):
        for e in range(len(order)):
            for k in range(n):
                for c in range(2):
                    from_lane = (2 * k + c) * lanes
                    value = late[e, :, from_lane : from_lane + own].astype(F32)
                    out[pl.ds(at[e], rows), pl.ds(c * DI + first(k), own)] = value

    if own % 128 == 0:
        put(lambda k: pl.multiple_of((me ^ k) * own, 128))
    else:
        for q in range(n):
            pl.when(me == q)(functools.partial(put, lambda k, q=q: (q ^ k) * own))
    for e in range(len(order)):
        out[pl.ds(at[e], rows), 2 * DI : 2 * DI + 2 * N] = late[e, :, late.shape[2] - 2 * N :].astype(F32)
    out[:, 2 * DI + 2 * N :] = step[:, :H]
    gain_o[...] = rows_dot(out[...], weight[...]) / gain[...]


def small_kernel(n, own_heads, scal, *refs):
    parts, (conv_o, step_o, heads_o), wide = refs[:n], refs[n : n + 3], refs[n + 3]
    own, rows = own_heads * PS, step_o.shape[0]
    lanes = own + own % 128
    width, chans = lanes + 2 * N, conv_o.shape[1]
    me = scal[0]
    for q in range(n):

        @pl.when(me == q)
        def _(q=q):
            shared, steps = jnp.zeros((8, 2 * N), F32), []
            for j in range(n):
                part = parts[q ^ j]
                wide[:, j * own : (j + 1) * own] = part[:, 0:own]
                shared = shared + part[:, lanes:width]
                first = width + 128 + q * rows
                steps.append(part[0:own_heads, first : first + rows])
            wide[:, DI:] = shared
            conv_o[...] = wide[:, q * chans : (q + 1) * chans]
            steps.append(jnp.zeros((128 - n * own_heads, rows), F32))
            step_o[...] = jnp.concatenate(steps, axis=0).T

    heads_o[...] = parts[0][:, width : width + 128]


def out_weight_kernel(order, scal, share, weight, gain, out, gain_o):
    rows = share.shape[1]
    for e, place in enumerate(order):
        at = 0 if len(order) == 1 else pl.multiple_of((place ^ scal[1]) * rows, 8)
        out[pl.ds(at, rows), :] = share[e].astype(F32)
    gain_o[...] = rows_dot(out[...], weight[...]) / gain[...]


def packets_kernel(n, own, scal, weight, *outs):
    for k in range(n):
        first = pl.multiple_of((scal[0] ^ k) * own, 128)
        outs[k][:, 0:own] = weight[:, pl.ds(DI + first, own)]
        outs[k][:, own:] = weight[:, pl.ds(first, own)]
    shared = outs[n]
    shared[:, 0 : 2 * N] = weight[:, 2 * DI : 2 * DI + 2 * N]
    shared[:, 2 * N :] = jnp.zeros((shared.shape[0], 128), BF)
    shared[:, 2 * N : 2 * N + H] = weight[:, 2 * DI + 2 * N :]


def xor(value, axis, k):
    return lax.ppermute(value, axis, [(s, s ^ k) for s in range(lax.axis_size(axis))])


def gather_xor(value, axis):
    out = [value]
    for k in range(1, lax.axis_size(axis)):
        out.append(xor(value, axis, k) if k % 2 == 0 or k == 1 else xor(out[k - 1], axis, 1))
    return out


def by_owner(parts, me):
    stacked = jnp.stack(parts)
    return [lax.dynamic_index_in_dim(stacked, me ^ j, 0, False) for j in range(len(parts))]


def stages(count):
    out, low = [], 0
    bits = count.bit_length() - 1
    while low < bits:
        take = 1 if low == 0 else min(2, bits - low)
        out.append((low, take))
        low += take
    return out


def gather_order(count):
    order = [0]
    for low, take in reversed(stages(count)):
        order = [o | (m << low) for m in range(1 << take) for o in order]
    return order


class Shares:
    def __init__(self, value, dim):
        self.value, self.dim = value, dim
        self.low = [low for low, _ in stages(value.shape[dim])]
        self.bits = dict(stages(value.shape[dim]))
        sizes = [1 << self.bits[low] for low in reversed(self.low)]
        self.value = value.reshape(value.shape[:dim] + tuple(sizes) + value.shape[dim + 1 :])
        self.left = list(reversed(self.low))

    def reduce(self, low):
        at = self.dim + self.left.index(low)
        take = lambda m: lax.index_in_dim(self.value, m, at, False)
        recv = [xor(take(m), "dp", m << low) for m in range(1, 1 << self.bits[low])]
        total = take(0).astype(F32)
        for part in recv:
            total = total + part.astype(F32)
        self.value = total.astype(BF)
        self.left.remove(low)


def gather_step(value, low, take):
    return jnp.concatenate([value] + [xor(value, "dp", m << low) for m in range(1, 1 << take)], 0)


def pair_step(value, hop):
    return jnp.concatenate([value, xor(value, "dp", hop)], 0)


def pair_order(count):
    order = [0]
    bits = [1 << bit for bit in range(count.bit_length() - 1)]
    for hop in bits[1:][::-1] + bits[:1]:
        order += [place | hop for place in order]
    return order


def tie(*values):
    return lax.optimization_barrier(values)


def call(
    kernel, name, grid, scal, in_specs, args, out_specs, out_shape, scratch, flops, bytes_, aliases={}
):
    return pl.pallas_call(
        kernel,
        grid_spec=pltpu.PrefetchScalarGridSpec(
            num_scalar_prefetch=1,
            grid=grid,
            in_specs=in_specs,
            out_specs=out_specs,
            scratch_shapes=scratch,
        ),
        out_shape=out_shape,
        name=name,
        input_output_aliases=aliases,
        compiler_params=pltpu.CompilerParams(vmem_limit_bytes=VMEM_LIMIT),
        cost_estimate=pl.CostEstimate(flops=flops, bytes_accessed=bytes_, transcendentals=0),
    )(scal, *args)


def local(
    block_input,
    out_cotangent,
    doc_lengths,
    norm_gain,
    in_weight,
    conv_weight,
    conv_bias,
    step_bias,
    decay_log,
    skip_gain,
    out_gain,
    out_weight,
):
    n, ndp = lax.axis_size("fsdp"), lax.axis_size("dp")
    me, dpi = lax.axis_index("fsdp"), lax.axis_index("dp")
    _, toks, model = block_input.shape
    length = toks * n
    nb = length // BLOCK
    own_heads = H // n
    heads = own_heads + own_heads % 2
    own, lanes = own_heads * PS, heads * PS
    width = lanes + 2 * N
    rows = model // n
    share = rows // ndp
    nd = ndp if share % 8 == 0 else 1
    x_own, g_own = block_input[0], out_cotangent[0]
    bounds = jnp.cumsum(doc_lengths[0])[:-1].astype(jnp.int32)
    scal = jnp.concatenate([jnp.stack([me, dpi]).astype(jnp.int32), bounds])

    def exchange(mine):
        return [mine[0]] + [xor(mine[k], "fsdp", k) for k in range(1, n)]

    xs = gather_xor(x_own, "fsdp")
    if own % 128 == 0:
        packets = call(
            functools.partial(packets_kernel, n, own),
            "packets",
            (1,),
            scal,
            [pl.BlockSpec(in_weight.shape, lambda b, s: (0, 0))],
            (in_weight,),
            [pl.BlockSpec((rows, 2 * own), lambda b, s: (0, 0))] * n
            + [pl.BlockSpec((rows, 2 * N + 128), lambda b, s: (0, 0))],
            [jax.ShapeDtypeStruct((rows, 2 * own), BF)] * n
            + [jax.ShapeDtypeStruct((rows, 2 * N + 128), BF)],
            [],
            10**6,
            3 * 10**6,
        )
        own_cols, shared = list(packets[:n]), packets[-1]
    else:

        def columns(first):
            part = in_weight[:, first : first + DI].reshape(rows, n, own).transpose(1, 0, 2)
            part = jnp.pad(part, ((0, 0), (0, 0), (0, lanes - own)))
            return [lax.dynamic_index_in_dim(part, me ^ k, 0, False) for k in range(n)]

        own_cols = [jnp.concatenate(both, axis=1) for both in zip(columns(DI), columns(0))]
        shared = jnp.pad(in_weight[:, 2 * DI :], ((0, 0), (0, 128 - H)))
    small = jnp.concatenate([norm_gain, conv_bias, conv_weight.reshape(-1)])
    small = jnp.pad(small, (0, -small.shape[0] % 1024)).reshape(-1, 128)
    shared, small = tie(shared, small)
    smalls = by_owner([small] + [xor(small, "fsdp", k) for k in range(1, n)], me)
    flat = jnp.stack(smalls).reshape(n, -1)
    chans = CONVCH // n
    gain_full = flat[:, :rows].reshape(1, model).astype(F32)
    conv_full = jnp.concatenate(
        [
            flat[:, rows + chans : rows + chans * (1 + KCONV)]
            .reshape(n, KCONV, chans)
            .transpose(1, 0, 2)
            .reshape(KCONV, CONVCH),
            flat[:, rows : rows + chans].reshape(1, CONVCH),
        ],
        axis=0,
    ).astype(F32)
    conv_heads = lax.dynamic_slice_in_dim(conv_full, me * own, own, 1)
    taps = jnp.concatenate(
        [jnp.pad(conv_heads, ((0, 0), (0, lanes - own))), conv_full[:, DI:]], axis=1
    )
    taps = jnp.pad(taps, ((0, 3), (0, 0)))
    hp = jnp.stack([step_bias, decay_log]).astype(F32)
    hp = jnp.pad(hp, ((0, 6), (0, 128 - own_heads)))
    skip = jnp.pad(jnp.repeat(skip_gain.astype(F32), PS), (0, lanes - own)).reshape(1, lanes)

    xs[2], *own_cols = tie(xs[2], *own_cols)
    xs[3] = xor(xs[2], "fsdp", 1)
    wks = gather_xor(shared, "fsdp")
    ws = exchange(own_cols)
    g_tied, *_ = tie(g_own, *ws[1:])
    gs = gather_xor(g_tied, "fsdp")

    any_spec = pl.BlockSpec(memory_space=ANY)

    def whole(*shape):
        return pl.BlockSpec(shape, lambda b, s: (0,) * len(shape))

    def tokens(cols):
        return pl.BlockSpec((BLOCK, cols), lambda b, s: (b, 0))

    shape = jax.ShapeDtypeStruct
    normed, normed_t, conv_in, convk_in, raw_step, mixer, starts = call(
        functools.partial(forward_kernel, n, heads, own_heads),
        "forward",
        (nb,),
        scal,
        [any_spec] * (3 * n) + [whole(1, model), whole(8, width), whole(8, 128), whole(1, lanes)],
        (*xs, *ws, *wks, gain_full, taps, hp, skip),
        [
            tokens(model),
            pl.BlockSpec((model, BLOCK), lambda b, s: (0, b)),
            tokens(lanes),
            tokens(2 * N),
            tokens(128),
            tokens(lanes),
            pl.BlockSpec((1, lanes, N), lambda b, s: (b, 0, 0)),
        ],
        [
            shape((length, model), BF),
            shape((model, length), BF),
            shape((length, lanes), BF),
            shape((length, 2 * N), BF),
            shape((length, 128), F32),
            shape((length, lanes), F32),
            shape((nb, lanes, N), F32),
        ],
        [
            pltpu.VMEM((length, model), BF),
            pltpu.VMEM((model, width + 128), BF),
            pltpu.VMEM((8 + BLOCK, width), F32),
            pltpu.VMEM((lanes, N), F32),
            pltpu.SemaphoreType.DMA((n,)),
            pltpu.SemaphoreType.DMA((n,)),
            pltpu.SemaphoreType.DMA((n,)),
        ],
        9 * 10**9,
        10**7,
    )

    gs[2], normed = tie(gs[2], normed)
    gs[3::2] = [xor(value, "fsdp", 1) for value in gs[2::2]]
    out_w = jnp.pad(out_weight, ((0, lanes - own), (0, 0)))
    out_g = jnp.pad(out_gain.astype(F32), (0, lanes - own)).reshape(1, lanes)
    raw_gate, gno, stat = call(
        functools.partial(gate_kernel, n),
        "gate",
        (nb,),
        scal,
        [any_spec] * (2 * n)
        + [tokens(model), tokens(lanes), whole(lanes, model), whole(1, lanes)],
        (*gs, *ws, normed, mixer, out_w, out_g),
        [tokens(lanes), tokens(lanes), pl.BlockSpec((8, BLOCK), lambda b, s: (0, b))],
        [
            shape((length, lanes), BF),
            shape((length, lanes), F32),
            shape((8, length), F32),
        ],
        [
            pltpu.VMEM((length, model), BF),
            pltpu.VMEM((model, lanes), BF),
            pltpu.SemaphoreType.DMA((n,)),
            pltpu.SemaphoreType.DMA((n,)),
        ],
        2 * 10**9,
        10**7,
    )
    side = max(1, model // lanes)
    early_count = lanes // nd + -(-n // side) * (rows // nd)
    stats = [stat] + [xor(stat, "fsdp", k) for k in range(1, n)]

    out_part, gssm, ggr, early = call(
        functools.partial(output_kernel, n, nd, DI),
        "output",
        (nb,),
        scal,
        [any_spec] * n
        + [pl.BlockSpec((8, BLOCK), lambda b, s: (0, b))] * n
        + [pl.BlockSpec((model, BLOCK), lambda b, s: (0, b))]
        + [tokens(lanes), tokens(lanes), tokens(lanes)]
        + [whole(lanes, model), whole(1, lanes)],
        (*gs, *stats, normed_t, mixer, raw_gate, gno, out_w, out_g),
        [
            pl.BlockSpec((1, BLOCK, model), lambda b, s: (b ^ s[0], 0, 0)),
            tokens(lanes),
            tokens(lanes),
            whole(nd, early_count, model),
        ],
        [
            shape((nb, BLOCK, model), BF),
            shape((length, lanes), BF),
            shape((length, lanes), BF),
            shape((nd, early_count, model), BF),
        ],
        [
            pltpu.VMEM((length, model), BF),
            pltpu.VMEM((lanes, model), F32),
            pltpu.VMEM((model, lanes), F32),
            pltpu.SemaphoreType.DMA((n,)),
        ],
        3 * 10**9,
        10**7,
    )

    def core_sum(parts):
        paired = parts.reshape(n // 2, 2, BLOCK, model)
        other = xor(paired[:, 1], "fsdp", 1)
        return (paired[:, 0].astype(F32) + other.astype(F32)).astype(BF)

    def chip_exchange(both):
        return both[0], [xor(both[k // 2], "fsdp", k) for k in range(2, n, 2)]

    def total_of(mine, recv):
        return functools.reduce(lambda a, c: a + c.astype(F32), recv, mine.astype(F32))

    def to_owners(shares):
        return [shares[0]] + [xor(shares[k], "fsdp", k) for k in range(1, n)]

    def late_rows(parts):
        shared_sum = functools.reduce(
            lambda a, c: a + c, [part[:, 2 * lanes :].astype(F32) for part in parts]
        )
        return jnp.concatenate(
            [part[:, : 2 * lanes] for part in parts] + [shared_sum.astype(BF)], axis=1
        )

    order = gather_order(ndp) if nd > 1 else [0]
    back = lambda b: nb - 1 - b

    def tokens_back(cols, at=0):
        return pl.BlockSpec((BLOCK, cols), lambda b, s: (back(b), at))

    def halo_back(cols, at=0):
        return pl.BlockSpec(
            (16, cols), lambda b, s: (jnp.maximum(back(b) * (BLOCK // 16) - 1, 0), at)
        )

    normed_back = pl.BlockSpec((model, BLOCK), lambda b, s: (0, back(b)))

    if nd > 1:
        early = Shares(early, 0)
        early.reduce(0)
    out_sum = core_sum(out_part)

    proj_low, dw, small_grads = call(
        functools.partial(scan_kernel, n, nd, heads, own_heads),
        "scan_back",
        (nb,),
        scal,
        [
            normed_back,
            tokens_back(lanes),
            halo_back(lanes),
            tokens_back(2 * N),
            halo_back(2 * N),
            tokens_back(128),
            pl.BlockSpec((1, lanes, N), lambda b, s: (back(b), 0, 0)),
            tokens_back(lanes),
            whole(8, width),
            whole(8, 128),
            whole(1, lanes),
        ],
        (
            normed_t,
            conv_in,
            conv_in,
            convk_in,
            convk_in,
            raw_step,
            starts,
            gssm,
            taps,
            hp,
            skip,
        ),
        [
            tokens_back(width + 128),
            whole(n, nd, rows // nd, width),
            whole(8, width + 128 + model),
        ],
        [
            shape((length, width + 128), BF),
            shape((n, nd, rows // nd, width), BF),
            shape((8, width + 128 + model), F32),
        ],
        [
            pltpu.VMEM((8 + BLOCK, width), F32),
            pltpu.VMEM((BLOCK + 8, width), F32),
            pltpu.VMEM((lanes, N), F32),
            pltpu.VMEM((model, width), F32),
            pltpu.VMEM((BLOCK, BLOCK), F32),
            pltpu.VMEM((lanes, BLOCK), F32),
        ],
        20 * 10**9,
        10**7,
    )
    if nd > 1:
        proj_low, dw, small_grads, early.value, out_sum = tie(
            proj_low, dw, small_grads, early.value, out_sum
        )
        late = Shares(dw, 1)
        late.reduce(0)
        for low in early.low[1:]:
            early.reduce(low)
        bits = [1 << bit for bit in range(ndp.bit_length() - 1)]
        small_grads = small_grads + xor(small_grads, "dp", bits[0])
    (gn_part,) = call(
        functools.partial(normed_kernel, n, lanes),
        "normed_grad",
        (nb,),
        scal,
        [any_spec] * (2 * n) + [tokens(width + 128), tokens(lanes)],
        (*ws, *wks, proj_low, ggr),
        [pl.BlockSpec((1, BLOCK, model), lambda b, s: (b ^ s[0], 0, 0))],
        [shape((nb, BLOCK, model), BF)],
        [
            pltpu.VMEM((model, width + 128), BF),
            pltpu.VMEM((model, lanes), BF),
            pltpu.SemaphoreType.DMA((n,)),
            pltpu.SemaphoreType.DMA((n,)),
            pltpu.SemaphoreType.DMA((n,)),
        ],
        5 * 10**9,
        10**7,
    )
    if nd > 1:
        gn_part, late.value, early.value, small_grads = tie(
            gn_part, late.value, early.value, small_grads
        )
        own_rows, part = lanes // nd, rows // nd
        wo, gates = early.value[:own_rows], early.value[own_rows:]
        for low in late.low[1:]:
            late.reduce(low)
        gn_mine, gn_recv = chip_exchange(core_sum(gn_part))
        late.value, wo, small_grads, *gn_recv = tie(late.value, wo, small_grads, *gn_recv)
        owned = to_owners(
            [
                jnp.concatenate(
                    [
                        gates[k // side * part : (k // side + 1) * part, k % side * lanes :][:, :lanes],
                        late.value[k],
                    ],
                    axis=1,
                )
                for k in range(n)
            ]
        )
        wo = wo[None]
        for hop in bits[1:][::-1]:
            wo = pair_step(wo, hop)
            small_grads = small_grads + xor(small_grads, "dp", hop)
        late = late_rows(owned)
        late, wo, small_grads = tie(late, wo, small_grads)
        gather = list(reversed(stages(ndp)))
        late = gather_step(late[None], *gather[0])
        wo = pair_step(wo, bits[0])
        small_other = xor(small_grads, "fsdp", 1)
        late, wo, small_other, out_sum = tie(late, wo, small_other, out_sum)
        for low, take in gather[1:]:
            late = gather_step(late, low, take)
        small_parts = [small_grads, small_other]
        for k in range(2, n, 2):
            pair = xor(jnp.concatenate([small_grads, small_other], axis=1), "fsdp", k)
            small_parts += [pair[:, : small_grads.shape[1]], pair[:, small_grads.shape[1] :]]
        out_mine, out_recv = chip_exchange(out_sum)
    else:
        out_mine, out_recv = chip_exchange(out_sum)
        gn_mine, gn_recv = chip_exchange(core_sum(gn_part))
        gates = [
            early[0, lanes + k // side * rows : lanes + (k // side + 1) * rows, k % side * lanes :][
                :, :lanes
            ]
            for k in range(n)
        ]
        owned = [jnp.concatenate([gates[k], dw[k, 0]], axis=1) for k in range(n)]
        late = lax.psum(late_rows(to_owners(owned)), "dp")[None]
        wo = lax.psum(early[0, :lanes], "dp")[None]
        small_parts = to_owners([lax.psum(small_grads, "dp")] * n)
    block_output = (x_own.astype(F32) + total_of(out_mine, out_recv)).astype(BF)[None]
    total_in = total_of(gn_mine, gn_recv)
    inputs = x_own.astype(F32)
    scale_in = lax.rsqrt(jnp.mean(inputs * inputs, axis=-1, keepdims=True) + EPS)
    gained = total_in * gain_full
    input_grad = scale_in * (
        gained - inputs * jnp.mean(gained * inputs, axis=-1, keepdims=True) * scale_in * scale_in
    ) + g_own.astype(F32)
    input_grad = input_grad.astype(BF)[None]

    conv_grads, step_cols, head_grads = call(
        functools.partial(small_kernel, n, own_heads),
        "small_grads",
        (1,),
        scal,
        [whole(*part.shape) for part in small_parts],
        small_parts,
        [whole(8, chans), whole(rows, 128), whole(8, 128)],
        [shape((8, chans), F32), shape((rows, 128), F32), shape((8, 128), F32)],
        [pltpu.VMEM((8, CONVCH), F32)],
        10**6,
        10**6,
    )
    head_grads = head_grads[:3, :own_heads]

    grad_in, grad_gain = call(
        functools.partial(weights_kernel, n, own, order),
        "in_weight_grad",
        (1,),
        scal,
        [
            whole(*late.shape),
            whole(rows, 128),
            whole(*in_weight.shape),
            whole(1, rows),
        ],
        (late, step_cols, in_weight, norm_gain.astype(F32).reshape(1, rows)),
        [whole(*in_weight.shape), whole(8, rows)],
        [shape(in_weight.shape, F32), shape((8, rows), F32)],
        [],
        10**8,
        6 * 10**6,
    )
    gain_ones = jnp.pad(out_gain.astype(F32), (0, lanes - own), constant_values=1.0)
    grad_out, grad_out_gain = call(
        functools.partial(out_weight_kernel, pair_order(ndp) if nd > 1 else [0]),
        "out_weight_grad",
        (1,),
        scal,
        [whole(*wo.shape), whole(lanes, model), whole(1, lanes)],
        (wo, out_w, gain_ones.reshape(1, lanes)),
        [whole(lanes, model), whole(8, lanes)],
        [shape((lanes, model), F32), shape((8, lanes), F32)],
        [],
        10**8,
        3 * 10**6,
    )
    return (
        block_output,
        input_grad,
        grad_gain[0],
        grad_in,
        conv_grads[:KCONV],
        conv_grads[KCONV],
        head_grads[0],
        head_grads[1],
        head_grads[2],
        grad_out_gain[0, :own],
        grad_out[:own],
    )


def solution(mesh):
    return jax.shard_map(
        local,
        mesh=mesh,
        in_specs=(
            P("dp", "fsdp", None),
            P("dp", "fsdp", None),
            P("dp", None),
            P("fsdp"),
            P("fsdp", None),
            P(None, "fsdp"),
            P("fsdp"),
            P("fsdp"),
            P("fsdp"),
            P("fsdp"),
            P("fsdp"),
            P("fsdp", None),
        ),
        out_specs=(
            P("dp", "fsdp", None),
            P("dp", "fsdp", None),
            P("fsdp"),
            P("fsdp", None),
            P(None, "fsdp"),
            P("fsdp"),
            P("fsdp"),
            P("fsdp"),
            P("fsdp"),
            P("fsdp"),
            P("fsdp", None),
        ),
        check_vma=False,
    )
```

```python
import functools

import jax
import jax.numpy as jnp
from jax import lax
from jax.experimental import pallas as pl
from jax.experimental.pallas import tpu as pltpu
from jax.sharding import PartitionSpec as P

H = 24
PS = 64
N = 128
KCONV = 4
BLOCK = 256
DI = 1536
CONVCH = 1792
EPS = 1e-05
BF = jnp.bfloat16
F32 = jnp.float32
ANY = pltpu.HBM
VMEM_LIMIT = 24 * 1024 * 1024
LIMITS = {"params": 4 << 20, "packets": 16 << 20}


def dot(a, b):
    return lax.dot_general(a, b, (((1,), (0,)), ((), ())), preferred_element_type=F32)


def dot_nt(a, b):
    return lax.dot_general(a, b, (((1,), (1,)), ((), ())), preferred_element_type=F32)


def dot_tn(a, b):
    return lax.dot_general(a, b, (((0,), (0,)), ((), ())), preferred_element_type=F32)


def pieces(value, count):
    out = []
    for _ in range(count):
        part = value.astype(BF)
        out.append(part)
        value = value - part.astype(F32)
    return out


def sigmoid(value):
    return 0.5 * jnp.tanh(0.5 * value) + 0.5


def iota(shape, dim):
    return lax.broadcasted_iota(jnp.int32, shape, dim)


def document_start(bounds, position):
    return functools.reduce(
        lambda start, bound: jnp.where(position >= bound, bound, start),
        bounds,
        jnp.zeros_like(position),
    )


def document_end(bounds, position):
    return functools.reduce(
        lambda end, bound: jnp.where(position < bound, bound, end),
        reversed(bounds),
        jnp.full_like(position, 1 << 30),
    )


def expand(table, pairs):
    low = iota((table.shape[0], 128), 1) < PS
    return jnp.concatenate(
        [
            jnp.where(low, table[:, 2 * p : 2 * p + 1], table[:, 2 * p + 1 : 2 * p + 2])
            for p in range(pairs)
        ],
        axis=1,
    )


def head_select(lanes):
    return (iota((lanes, 128), 0) // PS == iota((lanes, 128), 1)).astype(BF)


def head_sum(value):
    select = head_select(value.shape[1])
    return sum(dot(part, select) for part in pieces(value, 2))


def head_rows(row, lanes):
    mine = iota((lanes, 128), 0) // PS == iota((lanes, 128), 1)
    return jnp.sum(jnp.where(mine, row, 0.0), axis=1, keepdims=True)


def load_blocks(refs, dest, me, rows, sem, col=None):
    copies = []
    for k, ref in enumerate(refs):
        at = pl.ds(pl.multiple_of((me ^ k) * rows, 16), rows)
        to = dest.at[at] if col is None else dest.at[at, pl.ds(col[0], col[2])]
        ref = ref if col is None else ref.at[:, pl.ds(col[1], col[2])]
        copies.append(pltpu.make_async_copy(ref, to, sem.at[k]))
    for copy in copies:
        copy.start()
    return copies


def wait_block(ref, dest, me, b, sem):
    at = pl.ds(pl.multiple_of(b * BLOCK, BLOCK), BLOCK)
    pltpu.make_async_copy(ref, dest.at[at], sem.at[b ^ me]).wait()
    return dest[at, :]


def conv_forward(cext, taps, bounds, start):
    position = start + iota((BLOCK, 1), 0)
    depth = position - document_start(bounds, position)
    masks, pre = [], taps[KCONV : KCONV + 1, :]
    for k in range(KCONV):
        back = KCONV - 1 - k
        taken = cext[pl.ds(8 - back, BLOCK), :]
        if back:
            masks.append(jnp.where(depth >= back, 1.0, 0.0))
            taken = taken * masks[-1]
        pre = pre + taps[k : k + 1, :] * taken
    return pre, masks + [None]


def scan_terms(raw, heads, bounds, start):
    z = raw + heads[0:1, :]
    step = jnp.maximum(z, 0.0) + jnp.log1p(jnp.exp(-jnp.abs(z)))
    rate = -jnp.exp(heads[1:2, :])
    log_decay = step * rate
    tri = (iota((BLOCK, BLOCK), 0) >= iota((BLOCK, BLOCK), 1)).astype(BF)
    cum = sum(dot(tri, part) for part in pieces(log_decay, 3))
    position = start + iota((BLOCK, 1), 0)
    first = document_start(bounds, position)
    last_first = document_start(bounds, start + BLOCK - 1)
    other = start + iota((BLOCK, BLOCK), 1)
    bias = jnp.where((other <= position) & (other >= first), 0.0, -1e30)
    tail = cum[BLOCK - 1 : BLOCK, :]
    enter = jnp.where(first < start, jnp.exp(cum), 0.0)
    end = jnp.where(position >= last_first, jnp.exp(tail - cum), 0.0)
    keep = jnp.where(last_first < start, jnp.exp(tail), 0.0)
    return z, step, rate, cum, bias, enter, end, keep


def forward_kernel(n, heads, own_heads, scal, *refs):
    xs, ws, wks = refs[:n], refs[n : 2 * n], refs[2 * n : 3 * n]
    gain, taps, hp, skip = refs[3 * n : 3 * n + 4]
    normed_o, normed_t_o, conv_o, convk_o, raw_o, mixer_o, start_o, w_o, wg_o = refs[3 * n + 4 : 3 * n + 13]
    xv, wv, cext, state, sem_o, sem_x, sem_w, sem_k, sem_g = refs[3 * n + 13 :]
    lanes = heads * PS
    width = lanes + 2 * N
    b = pl.program_id(0)
    bounds = [scal[i] for i in range(2, scal.shape[0])]
    start = b * BLOCK

    @pl.when(b == 0)
    def _():
        me = scal[0]
        load_blocks(xs, xv, me, BLOCK, sem_x)
        copies = load_blocks(ws, wv, me, ws[0].shape[0], sem_w, (0, 0, lanes))
        copies += load_blocks(wks, wv, me, ws[0].shape[0], sem_k, (lanes, 0, 2 * N + 128))
        load_blocks(ws, wg_o, me, ws[0].shape[0], sem_g, (0, lanes, lanes))
        cext[0:8, :] = jnp.zeros((8, width), F32)
        state[...] = jnp.zeros_like(state)
        for copy in copies:
            copy.wait()
        pltpu.make_async_copy(wv, w_o, sem_o).start()

    @pl.when(b == pl.num_programs(0) - 1)
    def _():
        rows = ws[0].shape[0]
        for k in range(n):
            to = wg_o.at[pl.ds(0, rows), pl.ds(0, lanes)]
            pltpu.make_async_copy(ws[k].at[:, pl.ds(lanes, lanes)], to, sem_g.at[k]).wait()
        pltpu.make_async_copy(wv, w_o, sem_o).wait()

    x = wait_block(xs[0], xv, scal[0], b, sem_x).astype(F32)
    scale = lax.rsqrt(jnp.mean(x * x, axis=1, keepdims=True) + EPS)
    normed = (x * scale * gain[...]).astype(BF)
    normed_o[...] = normed
    normed_t_o[...] = normed.T
    proj = dot(normed, wv[...]).astype(BF)
    conv_o[...] = proj[:, :lanes]
    convk_o[...] = proj[:, lanes:width]
    raw = pltpu.roll(proj[:, width:].astype(F32), 128 - scal[0] * own_heads, 1)
    raw_o[...] = raw
    cext[8:, :] = proj[:, :width].astype(F32)
    pre, _ = conv_forward(cext, taps, bounds, start)
    cext[0:8, :] = cext[BLOCK:, :]
    act = pre * sigmoid(pre)
    low = act.astype(BF)
    full = act[:, :lanes]
    keys, query = low[:, lanes : lanes + N], low[:, lanes + N :]
    _, step, _, cum, bias, enter, end, keep = scan_terms(raw, hp, bounds, start)
    cum_t, step_t = cum.T, step.T
    gram = dot_nt(query, keys)
    start_state = state[...]
    start_o[0] = start_state
    inter = dot_nt(query, start_state.astype(BF)) * expand(enter, heads // 2)
    weighted = (full * expand(end * step, heads // 2)).astype(BF)
    state[...] = head_rows(keep, lanes) * start_state + dot_tn(weighted, keys)
    rest = inter + skip[...] * full
    first = iota((BLOCK, 2 * PS), 1) < PS
    for p in range(heads // 2):
        at = slice(2 * PS * p, 2 * PS * (p + 1))
        pair = low[:, at]
        halves = (jnp.where(first, pair, 0), jnp.where(first, 0, pair))
        for t in range(2):
            rows, cols = slice(128 * t, 128 * (t + 1)), slice(0, 128 * (t + 1))
            total = rest[rows, at]
            for i in range(2):
                h = 2 * p + i
                decay = jnp.exp(cum[rows, h : h + 1] - cum_t[h : h + 1, cols] + bias[rows, cols])
                weights = (gram[rows, cols] * decay * step_t[h : h + 1, cols]).astype(BF)
                total = total + dot(weights, halves[i][cols, :])
            mixer_o[rows, at] = total


def gate_kernel(n, scal, *refs):
    gs = refs[:n]
    wv, normed, mixer, wo, gain, raw_o, stat_o, gv, sem_g = refs[n:]
    b = pl.program_id(0)

    @pl.when(b == 0)
    def _():
        load_blocks(gs, gv, scal[0], BLOCK, sem_g)

    raw = dot(normed[...], wv[...]).astype(BF)
    raw_o[...] = raw
    gate = raw.astype(F32)
    gated = mixer[...] * (gate * sigmoid(gate))
    g = wait_block(gs[0], gv, scal[0], b, sem_g)
    gno = dot_nt(g, wo[...])
    first = jnp.sum(gated * gated, axis=1, keepdims=True)
    second = jnp.sum(gno * gain[...] * gated, axis=1, keepdims=True)
    lane = iota((BLOCK, 128), 1)
    both = jnp.where(lane == 0, first, jnp.where(lane == 1, second, 0.0))
    stat_o[...] = both.T[0:8, :]


def output_kernel(n, nd, inner, scal, *refs):
    gs = refs[:n]
    stats = refs[n : 2 * n]
    normed_t, mixer, raw, wo, gain = refs[2 * n : 2 * n + 5]
    out_o, gssm_o, ggr_o, early_o = refs[2 * n + 5 : 2 * n + 9]
    gv, acc_o, acc_g, sem_g = refs[2 * n + 9 :]
    b = pl.program_id(0)

    @pl.when(b == 0)
    def _():
        load_blocks(gs, gv, scal[0], BLOCK, sem_g)
        acc_o[...] = jnp.zeros_like(acc_o)
        acc_g[...] = jnp.zeros_like(acc_g)

    stat = functools.reduce(lambda a, c: a + c, [s[...] for s in stats])
    stat = jnp.concatenate([stat, jnp.zeros((120, BLOCK), F32)], axis=0).T
    scale = lax.rsqrt(stat[:, 0:1] * (1.0 / inner) + EPS)
    mean = stat[:, 1:2] * (1.0 / inner)
    mix = mixer[...]
    gate = raw[...].astype(F32)
    sig = sigmoid(gate)
    act = gate * sig
    gated = mix * act
    normed_out = (gated * scale * gain[...]).astype(BF)
    g = wait_block(gs[0], gv, scal[0], b, sem_g)
    out_o[0] = dot(normed_out, wo[...]).astype(BF)
    acc_o[...] += dot_tn(normed_out, g)
    grad_gated = scale * (dot_nt(g, wo[...]) * gain[...] - gated * (mean * scale * scale))
    grad_raw = (grad_gated * mix * (sig * (1.0 + gate * (1.0 - sig)))).astype(BF)
    ggr_o[...] = grad_raw
    gssm_o[...] = (grad_gated * act).astype(BF)
    acc_g[...] += dot(normed_t[...], grad_raw)

    @pl.when(b == pl.num_programs(0) - 1)
    def _():
        share, lanes, model = acc_o.shape[0] // nd, acc_g.shape[1], acc_o.shape[1]
        rows = model // n
        part, side = rows // nd, max(1, model // lanes)
        for d in range(nd):
            to = d ^ scal[1] if nd > 1 else d
            early_o[to, 0:share, :] = acc_o[d * share : (d + 1) * share, :].astype(BF)
            for j in range(n):
                k = j ^ scal[0]
                first = pl.multiple_of(share + k // side * part, 8)
                value = acc_g[j * rows + d * part : j * rows + (d + 1) * part, :].astype(BF)
                for c in range(side):

                    @pl.when(k % side == c)
                    def _(c=c, value=value, first=first, to=to):
                        early_o[to, pl.ds(first, part), c * lanes : (c + 1) * lanes] = value


def store_shares(acc, out, n, nd, scal):
    rows = acc.shape[0] // n
    share = rows // nd
    for j in range(n):
        for d in range(nd):
            at = j * rows + d * share
            out[j ^ scal[0], d ^ scal[1] if nd > 1 else d] = acc[at : at + share, :].astype(BF)


def scan_kernel(n, nd, heads, own_heads, scal, *refs):
    normed_t, conv, conv_before, convk, convk_before, raw, starts, gssm, taps, hp, skip = refs[:11]
    proj_o, dw_o, small_o = refs[11:14]
    cext, gext, end_grad, acc, ggram, ght = refs[14:]
    lanes = heads * PS
    width = lanes + 2 * N
    i = pl.program_id(0)
    b = pl.num_programs(0) - 1 - i
    bounds = [scal[k] for k in range(2, scal.shape[0])]
    start = b * BLOCK
    pairs = heads // 2

    @pl.when(i == 0)
    def _():
        gext[BLOCK:, :] = jnp.zeros((8, width), F32)
        end_grad[...] = jnp.zeros_like(end_grad)
        acc[...] = jnp.zeros_like(acc)
        small_o[...] = jnp.zeros_like(small_o)

    for source, halo, at in ((conv, conv_before, slice(0, lanes)), (convk, convk_before, slice(lanes, width))):
        cext[0:8, at] = jnp.where(b > 0, halo[8:16, :].astype(F32), 0.0)
        cext[8:, at] = source[...].astype(F32)
    pre, masks = conv_forward(cext, taps, bounds, start)
    sig = sigmoid(pre)
    act = pre * sig
    low = act.astype(BF)
    full = act[:, :lanes]
    keys, query = low[:, lanes : lanes + N], low[:, lanes + N :]
    z, step, rate, cum, bias, enter, end, keep = scan_terms(raw[...], hp, bounds, start)
    cum_t, step_t, enter_t = cum.T, step.T, enter.T
    gram = dot_nt(query, keys)
    grad = gssm[...]
    grad_f = grad.astype(F32)
    grad_t = grad_f.T.astype(BF)
    first = iota((BLOCK, 2 * PS), 1) < PS
    lane = iota((128, 128), 1)
    row_totals = [jnp.zeros((128, 128), F32), jnp.zeros((128, 128), F32)]
    col_totals = []
    ggram[...] = jnp.zeros_like(ggram)
    for p in range(pairs):
        at = slice(2 * PS * p, 2 * PS * (p + 1))
        pair = low[:, at]
        halves = (jnp.where(first, pair, 0), jnp.where(first, 0, pair))
        for k in range(2):
            h = 2 * p + k
            own = slice(PS * h, PS * (h + 1))
            cols_total = None
            for t in range(2):
                rows, cols = slice(128 * t, 128 * (t + 1)), slice(0, 128 * (t + 1))
                decay = jnp.exp(cum[rows, h : h + 1] - cum_t[h : h + 1, cols] + bias[rows, cols])
                table = dot_nt(grad[rows, at], halves[k][cols, :])
                gram_here = gram[rows, cols]
                step_row = step_t[h : h + 1, cols]
                weights = (gram_here * decay * step_row).astype(BF)
                common = table * decay
                stepped = common * step_row
                ggram[rows, cols] += stepped
                col = jnp.sum(common * gram_here, axis=0, keepdims=True)
                total = jnp.sum(stepped * gram_here, axis=1, keepdims=True)
                row_totals[t] = jnp.where(lane == h, total, row_totals[t])
                part = dot(grad_t[own, rows], weights)
                if t == 0:
                    ght[own, 0:128] = part
                    cols_total = col
                else:
                    ght[own, 0:128] += part[:, 0:128]
                    ght[own, 128:256] = part[:, 128:256]
                    cols_total = col + jnp.concatenate(
                        [cols_total, jnp.zeros((1, 128), F32)], axis=1
                    )
            col_totals.append(cols_total)
    col_totals.append(jnp.zeros((128 - heads, BLOCK), F32))
    grad_step = jnp.concatenate(col_totals, axis=0).T
    grad_cum = jnp.concatenate(row_totals, axis=0) - step * grad_step
    gg = ggram[...].astype(BF)
    start_state = starts[0]
    start_low = start_state.astype(BF)
    grad_cum += head_sum(grad_f * dot_nt(query, start_low)) * enter
    entered = (grad_f * expand(enter, pairs)).astype(BF)
    grad_query = dot(gg, keys) + dot(entered, start_low)
    later = end_grad[...]
    end_low = later.astype(BF)
    scaled = end * step
    scaled_wide = expand(scaled, pairs)
    weighted = (full * scaled_wide).astype(BF)
    grad_weighted = dot_nt(keys, end_low)
    grad_keys = dot_tn(gg, query) + dot(weighted, end_low)
    grad_end = head_sum(grad_weighted * full)
    grad_step += grad_end * end
    end_terms = grad_end * scaled
    ones = jnp.ones((8, N), BF)
    held = sum(dot_nt(ones, part) for part in pieces(later * start_state, 2))
    grad_tail = jnp.sum(end_terms, axis=0, keepdims=True) + head_sum(held)[0:1, :] * keep
    final = iota((BLOCK, 1), 0) == BLOCK - 1
    grad_cum = grad_cum - end_terms + jnp.where(final, grad_tail, 0.0)
    upper = (iota((BLOCK, BLOCK), 0) <= iota((BLOCK, BLOCK), 1)).astype(BF)
    grad_log = sum(dot(upper, part) for part in pieces(grad_cum, 3))
    grad_step += grad_log * rate
    grad_rate = jnp.sum(grad_log * step, axis=0, keepdims=True)
    grad_heads = ght[...].T + grad_weighted * scaled_wide + grad_f * skip[...]
    grad_skip = jnp.sum(grad_f * full, axis=0, keepdims=True)
    grad_act = jnp.concatenate([grad_heads, grad_keys, grad_query], axis=1)
    grad_pre = grad_act * (sig * (1.0 + pre * (1.0 - sig)))
    conv_low = conv_backward(grad_pre, gext, cext, masks, taps, bounds, start, small_o).astype(BF)
    grad_raw = grad_step * sigmoid(z)
    small_o[0:1, width : width + 128] += jnp.sum(grad_raw, axis=0, keepdims=True)
    small_o[1:2, width : width + 128] += grad_rate * rate
    small_o[2:3, width : width + 128] += head_sum(jnp.broadcast_to(grad_skip, (8, lanes)))[0:1, :]
    here = normed_t[...]
    raw_low = grad_raw.astype(BF)
    small_o[:, width + 128 :] += dot_nt(raw_low.T[0:16, :], here)[0:8, :]
    acc[...] += dot(here, conv_low)
    proj_o[:, :width] = conv_low
    proj_o[:, width:] = pltpu.roll(grad_raw, scal[0] * own_heads, 1).astype(BF)
    geared = jnp.concatenate(
        [grad_t[PS * h : PS * (h + 1), :].astype(F32) * enter_t[h : h + 1, :] for h in range(heads)],
        axis=0,
    ).astype(BF)
    end_grad[...] = head_rows(keep, lanes) * later + dot(geared, query)

    @pl.when(i == pl.num_programs(0) - 1)
    def _():
        store_shares(acc, dw_o, n, nd, scal)


def conv_backward(grad_pre, gext, cext, masks, taps, bounds, start, small_o):
    count = grad_pre.shape[1]
    gext[0:BLOCK, :] = grad_pre
    position = start + iota((BLOCK, 1), 0)
    left = document_end(bounds, position) - position
    total = None
    for k in range(KCONV):
        back = KCONV - 1 - k
        taken = cext[pl.ds(8 - back, BLOCK), :]
        after = gext[pl.ds(back, BLOCK), :]
        if back:
            taken = taken * masks[k]
            after = after * jnp.where(left > back, 1.0, 0.0)
        small_o[k : k + 1, 0:count] += jnp.sum(grad_pre * taken, axis=0, keepdims=True)
        term = taps[k : k + 1, :] * after
        total = term if total is None else total + term
    small_o[4:5, 0:count] += jnp.sum(grad_pre, axis=0, keepdims=True)
    gext[BLOCK:, :] = gext[0:8, :]
    return total


def normed_kernel(scal, proj, ggr, wv, wgv, gn_o):
    gn_o[0] = (dot_nt(proj[...], wv[...]) + dot_nt(ggr[...], wgv[...])).astype(BF)


def rows_dot(value, weight):
    product = value * weight.astype(F32)
    ones = jnp.ones((8, product.shape[1]), BF)
    return sum(dot_nt(ones, part) for part in pieces(product, 2))


def weights_kernel(n, own, order, scal, *refs):
    late, step, weight, gain, out, gain_o = refs
    rows, lanes = late.shape[1], (late.shape[2] - 2 * N) // (2 * n)
    me = scal[0]
    at = [
        0 if len(order) == 1 else pl.multiple_of((place ^ scal[1]) * rows, 8) for place in order
    ]

    def put(first):
        for e in range(len(order)):
            for k in range(n):
                for c in range(2):
                    from_lane = (2 * k + c) * lanes
                    value = late[e, :, from_lane : from_lane + own].astype(F32)
                    out[pl.ds(at[e], rows), pl.ds(c * DI + first(k), own)] = value

    if own % 128 == 0:
        put(lambda k: pl.multiple_of((me ^ k) * own, 128))
    else:
        for q in range(n):
            pl.when(me == q)(functools.partial(put, lambda k, q=q: (q ^ k) * own))
    for e in range(len(order)):
        out[pl.ds(at[e], rows), 2 * DI : 2 * DI + 2 * N] = late[e, :, late.shape[2] - 2 * N :].astype(F32)
    out[:, 2 * DI + 2 * N :] = step[:, :H]
    gain_o[...] = rows_dot(out[...], weight[...]) / gain[...]


def small_kernel(n, own_heads, scal, *refs):
    parts, (conv_o, step_o, heads_o), wide = refs[:n], refs[n : n + 3], refs[n + 3]
    own, rows = own_heads * PS, step_o.shape[0]
    lanes = own + own % 128
    width, chans = lanes + 2 * N, conv_o.shape[1]
    me = scal[0]
    for q in range(n):

        @pl.when(me == q)
        def _(q=q):
            shared, steps = jnp.zeros((8, 2 * N), F32), []
            for j in range(n):
                part = parts[q ^ j]
                wide[:, j * own : (j + 1) * own] = part[:, 0:own]
                shared = shared + part[:, lanes:width]
                first = width + 128 + q * rows
                steps.append(part[0:own_heads, first : first + rows])
            wide[:, DI:] = shared
            conv_o[...] = wide[:, q * chans : (q + 1) * chans]
            steps.append(jnp.zeros((128 - n * own_heads, rows), F32))
            step_o[...] = jnp.concatenate(steps, axis=0).T

    heads_o[...] = parts[0][:, width : width + 128]


def out_weight_kernel(order, scal, share, weight, gain, out, gain_o):
    rows = share.shape[1]
    for e, place in enumerate(order):
        at = 0 if len(order) == 1 else pl.multiple_of((place ^ scal[1]) * rows, 8)
        out[pl.ds(at, rows), :] = share[e].astype(F32)
    gain_o[...] = rows_dot(out[...], weight[...]) / gain[...]


def params_kernel(n, own_heads, scal, *refs):
    parts, (gain_o, taps_o, wide) = refs[:n], refs[n:]
    own = own_heads * PS
    lanes, chans, rows = own + own % 128, CONVCH // n, gain_o.shape[1] // n
    for q in range(n):

        @pl.when(scal[0] == q)
        def _(q=q):
            for j in range(n):
                part = parts[q ^ j][...].astype(F32)
                gain_o[:, j * rows : (j + 1) * rows] = part[0:1, 0:rows]
                wide[:, j * chans : (j + 1) * chans] = part[:, 0:chans]
            taps_o[...] = jnp.zeros(taps_o.shape, F32)
            for to, at, size in ((0, q * own, own), (lanes, DI, 2 * N)):
                taps_o[0:KCONV, to : to + size] = wide[2 : 2 + KCONV, at : at + size]
                taps_o[KCONV : KCONV + 1, to : to + size] = wide[1:2, at : at + size]


def packets_kernel(n, own, scal, weight, *outs):
    for k in range(n):
        first = pl.multiple_of((scal[0] ^ k) * own, 128)
        outs[k][:, 0:own] = weight[:, pl.ds(DI + first, own)]
        outs[k][:, own:] = weight[:, pl.ds(first, own)]
    shared = outs[n]
    shared[:, 0 : 2 * N] = weight[:, 2 * DI : 2 * DI + 2 * N]
    shared[:, 2 * N :] = jnp.zeros((shared.shape[0], 128), BF)
    shared[:, 2 * N : 2 * N + H] = weight[:, 2 * DI + 2 * N :]


def xor(value, axis, k):
    return lax.ppermute(value, axis, [(s, s ^ k) for s in range(lax.axis_size(axis))])


def gather_xor(value, axis):
    out = [value]
    for k in range(1, lax.axis_size(axis)):
        out.append(xor(value, axis, k) if k % 2 == 0 or k == 1 else xor(out[k - 1], axis, 1))
    return out


def by_owner(parts, me):
    stacked = jnp.stack(parts)
    return [lax.dynamic_index_in_dim(stacked, me ^ j, 0, False) for j in range(len(parts))]


def stages(count):
    out, low = [], 0
    bits = count.bit_length() - 1
    while low < bits:
        take = 1 if low == 0 else min(2, bits - low)
        out.append((low, take))
        low += take
    return out


def gather_order(count):
    order = [0]
    for low, take in reversed(stages(count)):
        order = [o | (m << low) for m in range(1 << take) for o in order]
    return order


class Shares:
    def __init__(self, value, dim):
        self.value, self.dim = value, dim
        self.low = [low for low, _ in stages(value.shape[dim])]
        self.bits = dict(stages(value.shape[dim]))
        sizes = [1 << self.bits[low] for low in reversed(self.low)]
        self.value = value.reshape(value.shape[:dim] + tuple(sizes) + value.shape[dim + 1 :])
        self.left = list(reversed(self.low))

    def reduce(self, low):
        at = self.dim + self.left.index(low)
        take = lambda m: lax.index_in_dim(self.value, m, at, False)
        recv = [xor(take(m), "dp", m << low) for m in range(1, 1 << self.bits[low])]
        total = take(0).astype(F32)
        for part in recv:
            total = total + part.astype(F32)
        self.value = total.astype(BF)
        self.left.remove(low)


def gather_step(value, low, take):
    return jnp.concatenate([value] + [xor(value, "dp", m << low) for m in range(1, 1 << take)], 0)


def pair_step(value, hop):
    return jnp.concatenate([value, xor(value, "dp", hop)], 0)


def pair_order(count):
    order = [0]
    bits = [1 << bit for bit in range(count.bit_length() - 1)]
    for hop in bits[1:][::-1] + bits[:1]:
        order += [place | hop for place in order]
    return order


def tie(*values):
    return lax.optimization_barrier(values)


def call(
    kernel, name, grid, scal, in_specs, args, out_specs, out_shape, scratch, flops, bytes_, aliases={}
):
    return pl.pallas_call(
        kernel,
        grid_spec=pltpu.PrefetchScalarGridSpec(
            num_scalar_prefetch=1,
            grid=grid,
            in_specs=in_specs,
            out_specs=out_specs,
            scratch_shapes=scratch,
        ),
        out_shape=out_shape,
        name=name,
        input_output_aliases=aliases,
        compiler_params=pltpu.CompilerParams(vmem_limit_bytes=LIMITS.get(name, VMEM_LIMIT)),
        cost_estimate=pl.CostEstimate(flops=flops, bytes_accessed=bytes_, transcendentals=0),
    )(scal, *args)


def local(
    block_input,
    out_cotangent,
    doc_lengths,
    norm_gain,
    in_weight,
    conv_weight,
    conv_bias,
    step_bias,
    decay_log,
    skip_gain,
    out_gain,
    out_weight,
):
    n, ndp = lax.axis_size("fsdp"), lax.axis_size("dp")
    me, dpi = lax.axis_index("fsdp"), lax.axis_index("dp")
    _, toks, model = block_input.shape
    length = toks * n
    nb = length // BLOCK
    own_heads = H // n
    heads = own_heads + own_heads % 2
    own, lanes = own_heads * PS, heads * PS
    width = lanes + 2 * N
    rows = model // n
    share = rows // ndp
    nd = ndp if share % 8 == 0 else 1
    x_own, g_own = block_input[0], out_cotangent[0]
    bounds = jnp.cumsum(doc_lengths[0])[:-1].astype(jnp.int32)
    scal = jnp.concatenate([jnp.stack([me, dpi]).astype(jnp.int32), bounds])

    def exchange(mine):
        return [mine[0]] + [xor(mine[k], "fsdp", k) for k in range(1, n)]

    xs = gather_xor(x_own, "fsdp")
    xs[1], packed_weight = tie(xs[1], in_weight)
    if own % 128 == 0:
        packets = call(
            functools.partial(packets_kernel, n, own),
            "packets",
            (1,),
            scal,
            [pl.BlockSpec(in_weight.shape, lambda b, s: (0, 0))],
            (packed_weight,),
            [pl.BlockSpec((rows, 2 * own), lambda b, s: (0, 0))] * n
            + [pl.BlockSpec((rows, 2 * N + 128), lambda b, s: (0, 0))],
            [jax.ShapeDtypeStruct((rows, 2 * own), BF)] * n
            + [jax.ShapeDtypeStruct((rows, 2 * N + 128), BF)],
            [],
            10**6,
            3 * 10**6,
        )
        own_cols, shared = list(packets[:n]), packets[-1]
    else:

        def columns(first):
            part = in_weight[:, first : first + DI].reshape(rows, n, own).transpose(1, 0, 2)
            part = jnp.pad(part, ((0, 0), (0, 0), (0, lanes - own)))
            return [lax.dynamic_index_in_dim(part, me ^ k, 0, False) for k in range(n)]

        own_cols = [jnp.concatenate(both, axis=1) for both in zip(columns(DI), columns(0))]
        shared = jnp.pad(in_weight[:, 2 * DI :], ((0, 0), (0, 128 - H)))
    chans = CONVCH // n
    pack = -(-max(rows, chans) // 128) * 128
    line = lambda value: jnp.pad(value, ((0, 0), (0, pack - value.shape[1])))
    small = jnp.concatenate(
        [line(norm_gain[None]), line(conv_bias[None]), line(conv_weight), jnp.zeros((2, pack), BF)]
    )
    xs[1], small = tie(xs[1], small)
    smalls = [small] + [xor(small, "fsdp", k) for k in range(1, n)]
    hp = jnp.stack([step_bias, decay_log]).astype(F32)
    hp = jnp.pad(hp, ((0, 6), (0, 128 - own_heads)))
    skip = jnp.pad(jnp.repeat(skip_gain.astype(F32), PS), (0, lanes - own)).reshape(1, lanes)

    out_w = jnp.pad(out_weight, ((0, lanes - own), (0, 0)))
    out_g = jnp.pad(out_gain.astype(F32), (0, lanes - own), constant_values=1.0).reshape(1, lanes)
    gain_row = norm_gain.astype(F32).reshape(1, rows)
    hp, skip, out_g, gain_row, scal, xs[2], *rest = tie(
        hp, skip, out_g, gain_row, scal, xs[2], *smalls[1:], *own_cols
    )
    smalls[1:], own_cols = rest[: n - 1], rest[n - 1 :]
    full = lambda *dims: pl.BlockSpec(dims, lambda b, s: (0,) * len(dims))
    gain_full, taps = call(
        functools.partial(params_kernel, n, own_heads),
        "params",
        (1,),
        scal,
        [full(8, pack)] * n,
        smalls,
        [full(1, model), full(8, width)],
        [jax.ShapeDtypeStruct((1, model), F32), jax.ShapeDtypeStruct((8, width), F32)],
        [pltpu.VMEM((8, CONVCH), F32)],
        10**6,
        10**5,
    )
    xs[3] = xor(xs[2], "fsdp", 1)
    wks = gather_xor(shared, "fsdp")
    ws = exchange(own_cols)
    g_tied, *_ = tie(g_own, *ws[1:])
    gs = gather_xor(g_tied, "fsdp")

    any_spec = pl.BlockSpec(memory_space=ANY)

    def whole(*shape):
        return pl.BlockSpec(shape, lambda b, s: (0,) * len(shape))

    def tokens(cols):
        return pl.BlockSpec((BLOCK, cols), lambda b, s: (b, 0))

    shape = jax.ShapeDtypeStruct
    normed, normed_t, conv_in, convk_in, raw_step, mixer, starts, w_conv, w_gate = call(
        functools.partial(forward_kernel, n, heads, own_heads),
        "forward",
        (nb,),
        scal,
        [any_spec] * (3 * n) + [whole(1, model), whole(8, width), whole(8, 128), whole(1, lanes)],
        (*xs, *ws, *wks, gain_full, taps, hp, skip),
        [
            tokens(model),
            pl.BlockSpec((model, BLOCK), lambda b, s: (0, b)),
            tokens(lanes),
            tokens(2 * N),
            tokens(128),
            tokens(lanes),
            pl.BlockSpec((1, lanes, N), lambda b, s: (b, 0, 0)),
            any_spec,
            any_spec,
        ],
        [
            shape((length, model), BF),
            shape((model, length), BF),
            shape((length, lanes), BF),
            shape((length, 2 * N), BF),
            shape((length, 128), F32),
            shape((length, lanes), F32),
            shape((nb, lanes, N), F32),
            shape((model, width + 128), BF),
            shape((model, lanes), BF),
        ],
        [
            pltpu.VMEM((length, model), BF),
            pltpu.VMEM((model, width + 128), BF),
            pltpu.VMEM((8 + BLOCK, width), F32),
            pltpu.VMEM((lanes, N), F32),
            pltpu.SemaphoreType.DMA,
            pltpu.SemaphoreType.DMA((n,)),
            pltpu.SemaphoreType.DMA((n,)),
            pltpu.SemaphoreType.DMA((n,)),
            pltpu.SemaphoreType.DMA((n,)),
        ],
        9 * 10**9,
        10**7,
    )

    gs[2], normed = tie(gs[2], normed)
    gs[3::2] = [xor(value, "fsdp", 1) for value in gs[2::2]]
    raw_gate, stat = call(
        functools.partial(gate_kernel, n),
        "gate",
        (nb,),
        scal,
        [any_spec] * n
        + [whole(model, lanes), tokens(model), tokens(lanes), whole(lanes, model), whole(1, lanes)],
        (*gs, w_gate, normed, mixer, out_w, out_g),
        [tokens(lanes), pl.BlockSpec((8, BLOCK), lambda b, s: (0, b))],
        [
            shape((length, lanes), BF),
            shape((8, length), F32),
        ],
        [
            pltpu.VMEM((length, model), BF),
            pltpu.SemaphoreType.DMA((n,)),
        ],
        2 * 10**9,
        10**7,
    )
    side = max(1, model // lanes)
    early_count = lanes // nd + -(-n // side) * (rows // nd)
    stats = [stat] + [xor(stat, "fsdp", k) for k in range(1, n)]

    out_part, gssm, ggr, early = call(
        functools.partial(output_kernel, n, nd, DI),
        "output",
        (nb,),
        scal,
        [any_spec] * n
        + [pl.BlockSpec((8, BLOCK), lambda b, s: (0, b))] * n
        + [pl.BlockSpec((model, BLOCK), lambda b, s: (0, b))]
        + [tokens(lanes), tokens(lanes)]
        + [whole(lanes, model), whole(1, lanes)],
        (*gs, *stats, normed_t, mixer, raw_gate, out_w, out_g),
        [
            pl.BlockSpec((1, BLOCK, model), lambda b, s: (b ^ s[0], 0, 0)),
            tokens(lanes),
            tokens(lanes),
            whole(nd, early_count, model),
        ],
        [
            shape((nb, BLOCK, model), BF),
            shape((length, lanes), BF),
            shape((length, lanes), BF),
            shape((nd, early_count, model), BF),
        ],
        [
            pltpu.VMEM((length, model), BF),
            pltpu.VMEM((lanes, model), F32),
            pltpu.VMEM((model, lanes), F32),
            pltpu.SemaphoreType.DMA((n,)),
        ],
        3 * 10**9,
        10**7,
    )

    def core_sum(parts):
        paired = parts.reshape(n // 2, 2, BLOCK, model)
        other = xor(paired[:, 1], "fsdp", 1)
        return (paired[:, 0].astype(F32) + other.astype(F32)).astype(BF)

    def chip_exchange(both):
        return both[0], [xor(both[k // 2], "fsdp", k) for k in range(2, n, 2)]

    def total_of(mine, recv):
        return functools.reduce(lambda a, c: a + c.astype(F32), recv, mine.astype(F32))

    def to_owners(shares):
        return [shares[0]] + [xor(shares[k], "fsdp", k) for k in range(1, n)]

    def late_rows(parts):
        shared_sum = functools.reduce(
            lambda a, c: a + c, [part[:, 2 * lanes :].astype(F32) for part in parts]
        )
        return jnp.concatenate(
            [part[:, : 2 * lanes] for part in parts] + [shared_sum.astype(BF)], axis=1
        )

    order = gather_order(ndp) if nd > 1 else [0]
    back = lambda b: nb - 1 - b

    def tokens_back(cols, at=0):
        return pl.BlockSpec((BLOCK, cols), lambda b, s: (back(b), at))

    def halo_back(cols, at=0):
        return pl.BlockSpec(
            (16, cols), lambda b, s: (jnp.maximum(back(b) * (BLOCK // 16) - 1, 0), at)
        )

    normed_back = pl.BlockSpec((model, BLOCK), lambda b, s: (0, back(b)))

    if nd > 1:
        early = Shares(early, 0)
        early.reduce(0)
    out_sum = core_sum(out_part)

    proj_low, dw, small_grads = call(
        functools.partial(scan_kernel, n, nd, heads, own_heads),
        "scan_back",
        (nb,),
        scal,
        [
            normed_back,
            tokens_back(lanes),
            halo_back(lanes),
            tokens_back(2 * N),
            halo_back(2 * N),
            tokens_back(128),
            pl.BlockSpec((1, lanes, N), lambda b, s: (back(b), 0, 0)),
            tokens_back(lanes),
            whole(8, width),
            whole(8, 128),
            whole(1, lanes),
        ],
        (
            normed_t,
            conv_in,
            conv_in,
            convk_in,
            convk_in,
            raw_step,
            starts,
            gssm,
            taps,
            hp,
            skip,
        ),
        [
            tokens_back(width + 128),
            whole(n, nd, rows // nd, width),
            whole(8, width + 128 + model),
        ],
        [
            shape((length, width + 128), BF),
            shape((n, nd, rows // nd, width), BF),
            shape((8, width + 128 + model), F32),
        ],
        [
            pltpu.VMEM((8 + BLOCK, width), F32),
            pltpu.VMEM((BLOCK + 8, width), F32),
            pltpu.VMEM((lanes, N), F32),
            pltpu.VMEM((model, width), F32),
            pltpu.VMEM((BLOCK, BLOCK), F32),
            pltpu.VMEM((lanes, BLOCK), F32),
        ],
        20 * 10**9,
        10**7,
    )
    if nd > 1:
        proj_low, dw, small_grads, early.value, out_sum = tie(
            proj_low, dw, small_grads, early.value, out_sum
        )
        late = Shares(dw, 1)
        late.reduce(0)
        for low in early.low[1:]:
            early.reduce(low)
        bits = [1 << bit for bit in range(ndp.bit_length() - 1)]
        small_grads = small_grads + xor(small_grads, "dp", bits[0])
    (gn_part,) = call(
        normed_kernel,
        "normed_grad",
        (nb,),
        scal,
        [tokens(width + 128), tokens(lanes), whole(model, width + 128), whole(model, lanes)],
        (proj_low, ggr, w_conv, w_gate),
        [pl.BlockSpec((1, BLOCK, model), lambda b, s: (b ^ s[0], 0, 0))],
        [shape((nb, BLOCK, model), BF)],
        [],
        5 * 10**9,
        10**7,
    )
    if nd > 1:
        gn_part, late.value, early.value, small_grads = tie(
            gn_part, late.value, early.value, small_grads
        )
        own_rows, part = lanes // nd, rows // nd
        wo, gates = early.value[:own_rows], early.value[own_rows:]
        for low in late.low[1:]:
            late.reduce(low)
        gn_mine, gn_recv = chip_exchange(core_sum(gn_part))
        hops = bits[1:][::-1]
        wo = pair_step(wo[None], hops[0])
        late.value, wo, small_grads = tie(late.value, wo, small_grads)
        owned = to_owners(
            [
                jnp.concatenate(
                    [
                        gates[k // side * part : (k // side + 1) * part, k % side * lanes :][:, :lanes],
                        late.value[k],
                    ],
                    axis=1,
                )
                for k in range(n)
            ]
        )
        for hop in hops[1:]:
            wo = pair_step(wo, hop)
        small_grads = small_grads + xor(small_grads, "dp", hops[0])
        late = late_rows(owned)
        late, wo, small_grads = tie(late, wo, small_grads)
        gather = list(reversed(stages(ndp)))
        late = gather_step(late[None], *gather[0])
        wo = pair_step(wo, bits[0])
        for hop in hops[1:]:
            small_grads = small_grads + xor(small_grads, "dp", hop)
        late, wo, small_grads, out_sum, *gn_recv = tie(late, wo, small_grads, out_sum, *gn_recv)
        for low, take in gather[1:]:
            late = gather_step(late, low, take)
        small_other = xor(small_grads, "fsdp", 1)
        small_parts = [small_grads, small_other]
        for k in range(2, n, 2):
            pair = xor(jnp.concatenate([small_grads, small_other], axis=1), "fsdp", k)
            small_parts += [pair[:, : small_grads.shape[1]], pair[:, small_grads.shape[1] :]]
        out_mine, out_recv = chip_exchange(out_sum)
    else:
        out_mine, out_recv = chip_exchange(out_sum)
        gn_mine, gn_recv = chip_exchange(core_sum(gn_part))
        gates = [
            early[0, lanes + k // side * rows : lanes + (k // side + 1) * rows, k % side * lanes :][
                :, :lanes
            ]
            for k in range(n)
        ]
        owned = [jnp.concatenate([gates[k], dw[k, 0]], axis=1) for k in range(n)]
        late = lax.psum(late_rows(to_owners(owned)), "dp")[None]
        wo = lax.psum(early[0, :lanes], "dp")[None]
        small_parts = to_owners([lax.psum(small_grads, "dp")] * n)
    block_output = (x_own.astype(F32) + total_of(out_mine, out_recv)).astype(BF)[None]
    total_in = total_of(gn_mine, gn_recv)
    inputs = x_own.astype(F32)
    scale_in = lax.rsqrt(jnp.mean(inputs * inputs, axis=-1, keepdims=True) + EPS)
    gained = total_in * gain_full
    input_grad = scale_in * (
        gained - inputs * jnp.mean(gained * inputs, axis=-1, keepdims=True) * scale_in * scale_in
    ) + g_own.astype(F32)
    input_grad = input_grad.astype(BF)[None]

    conv_grads, step_cols, head_grads = call(
        functools.partial(small_kernel, n, own_heads),
        "small_grads",
        (1,),
        scal,
        [whole(*part.shape) for part in small_parts],
        small_parts,
        [whole(8, chans), whole(rows, 128), whole(8, 128)],
        [shape((8, chans), F32), shape((rows, 128), F32), shape((8, 128), F32)],
        [pltpu.VMEM((8, CONVCH), F32)],
        10**6,
        10**6,
    )
    head_grads = head_grads[:3, :own_heads]

    grad_in, grad_gain = call(
        functools.partial(weights_kernel, n, own, order),
        "in_weight_grad",
        (1,),
        scal,
        [
            whole(*late.shape),
            whole(rows, 128),
            whole(*in_weight.shape),
            whole(1, rows),
        ],
        (late, step_cols, in_weight, gain_row),
        [whole(*in_weight.shape), whole(8, rows)],
        [shape(in_weight.shape, F32), shape((8, rows), F32)],
        [],
        10**8,
        6 * 10**6,
    )
    grad_out, grad_out_gain = call(
        functools.partial(out_weight_kernel, pair_order(ndp) if nd > 1 else [0]),
        "out_weight_grad",
        (1,),
        scal,
        [whole(*wo.shape), whole(lanes, model), whole(1, lanes)],
        (wo, out_w, out_g),
        [whole(lanes, model), whole(8, lanes)],
        [shape((lanes, model), F32), shape((8, lanes), F32)],
        [],
        10**8,
        3 * 10**6,
    )
    return (
        block_output,
        input_grad,
        grad_gain[0],
        grad_in,
        conv_grads[:KCONV],
        conv_grads[KCONV],
        head_grads[0],
        head_grads[1],
        head_grads[2],
        grad_out_gain[0, :own],
        grad_out[:own],
    )


def solution(mesh):
    return jax.shard_map(
        local,
        mesh=mesh,
        in_specs=(
            P("dp", "fsdp", None),
            P("dp", "fsdp", None),
            P("dp", None),
            P("fsdp"),
            P("fsdp", None),
            P(None, "fsdp"),
            P("fsdp"),
            P("fsdp"),
            P("fsdp"),
            P("fsdp"),
            P("fsdp"),
            P("fsdp", None),
        ),
        out_specs=(
            P("dp", "fsdp", None),
            P("dp", "fsdp", None),
            P("fsdp"),
            P("fsdp", None),
            P(None, "fsdp"),
            P("fsdp"),
            P("fsdp"),
            P("fsdp"),
            P("fsdp"),
            P("fsdp"),
            P("fsdp", None),
        ),
        check_vma=False,
    )
```

```python
import functools

import jax
import jax.numpy as jnp
from jax import lax
from jax.experimental import pallas as pl
from jax.experimental.pallas import tpu as pltpu
from jax.sharding import PartitionSpec as P

H = 24
PS = 64
N = 128
KCONV = 4
BLOCK = 256
PAIR = 2
DI = 1536
CONVCH = 1792
EPS = 1e-05
BF = jnp.bfloat16
F32 = jnp.float32
ANY = pltpu.HBM
VMEM_LIMIT = 24 * 1024 * 1024
LIMITS = {"params": 4 << 20, "packets": 16 << 20}


def dot(a, b):
    return lax.dot_general(a, b, (((1,), (0,)), ((), ())), preferred_element_type=F32)


def dot_nt(a, b):
    return lax.dot_general(a, b, (((1,), (1,)), ((), ())), preferred_element_type=F32)


def dot_tn(a, b):
    return lax.dot_general(a, b, (((0,), (0,)), ((), ())), preferred_element_type=F32)


def pieces(value, count):
    out = []
    for _ in range(count):
        part = value.astype(BF)
        out.append(part)
        value = value - part.astype(F32)
    return out


def sigmoid(value):
    return 0.5 * jnp.tanh(0.5 * value) + 0.5


def iota(shape, dim):
    return lax.broadcasted_iota(jnp.int32, shape, dim)


def document_start(bounds, position):
    return functools.reduce(
        lambda start, bound: jnp.where(position >= bound, bound, start),
        bounds,
        jnp.zeros_like(position),
    )


def document_end(bounds, position):
    return functools.reduce(
        lambda end, bound: jnp.where(position < bound, bound, end),
        reversed(bounds),
        jnp.full_like(position, 1 << 30),
    )


def expand(table, pairs):
    lanes = 2 * PS * pairs
    select = (iota((128, lanes), 0) == iota((128, lanes), 1) // PS).astype(BF)
    return sum(dot(part, select) for part in pieces(table, 2))


def head_select(lanes):
    return (iota((lanes, 128), 0) // PS == iota((lanes, 128), 1)).astype(BF)


def head_sum(value):
    select = head_select(value.shape[1])
    return sum(dot(part, select) for part in pieces(value, 2))


def head_rows(row, lanes):
    mine = iota((lanes, 128), 0) // PS == iota((lanes, 128), 1)
    return jnp.sum(jnp.where(mine, row, 0.0), axis=1, keepdims=True)


def load_blocks(refs, dest, me, rows, sem, col=None):
    copies = []
    for k, ref in enumerate(refs):
        at = pl.ds(pl.multiple_of((me ^ k) * rows, 16), rows)
        to = dest.at[at] if col is None else dest.at[at, pl.ds(col[0], col[2])]
        ref = ref if col is None else ref.at[:, pl.ds(col[1], col[2])]
        copies.append(pltpu.make_async_copy(ref, to, sem.at[k]))
    for copy in copies:
        copy.start()
    return copies


def wait_block(ref, dest, me, b, sem):
    at = pl.ds(pl.multiple_of(b * BLOCK, BLOCK), BLOCK)
    pltpu.make_async_copy(ref, dest.at[at], sem.at[b ^ me]).wait()
    return dest[at, :]


def conv_forward(cext, taps, bounds, start):
    position = start + iota((BLOCK, 1), 0)
    depth = position - document_start(bounds, position)
    masks, pre = [], taps[KCONV : KCONV + 1, :]
    for k in range(KCONV):
        back = KCONV - 1 - k
        taken = cext[pl.ds(8 - back, BLOCK), :]
        if back:
            masks.append(jnp.where(depth >= back, 1.0, 0.0))
            taken = taken * masks[-1]
        pre = pre + taps[k : k + 1, :] * taken
    return pre, masks + [None]


def scan_terms(raw, heads, bounds, start):
    z = raw + heads[0:1, :]
    step = jnp.maximum(z, 0.0) + jnp.log1p(jnp.exp(-jnp.abs(z)))
    rate = -jnp.exp(heads[1:2, :])
    log_decay = step * rate
    tri = (iota((BLOCK, BLOCK), 0) >= iota((BLOCK, BLOCK), 1)).astype(BF)
    cum = sum(dot(tri, part) for part in pieces(log_decay, 3))
    position = start + iota((BLOCK, 1), 0)
    first = document_start(bounds, position)
    last_first = document_start(bounds, start + BLOCK - 1)
    other = start + iota((BLOCK, BLOCK), 1)
    bias = jnp.where((other <= position) & (other >= first), 0.0, -1e30)
    tail = cum[BLOCK - 1 : BLOCK, :]
    enter = jnp.where(first < start, jnp.exp(cum), 0.0)
    end = jnp.where(position >= last_first, jnp.exp(tail - cum), 0.0)
    keep = jnp.where(last_first < start, jnp.exp(tail), 0.0)
    return z, step, rate, cum, bias, enter, end, keep


def forward_kernel(n, heads, own_heads, scal, *refs):
    xs, ws, wks = refs[:n], refs[n : 2 * n], refs[2 * n : 3 * n]
    gain, taps, hp, skip = refs[3 * n : 3 * n + 4]
    normed_o, normed_t_o, conv_o, convk_o, raw_o, mixer_o, start_o, w_o, wg_o = refs[3 * n + 4 : 3 * n + 13]
    xv, wv, cext, state, sem_o, sem_x, sem_w, sem_k, sem_g = refs[3 * n + 13 :]
    lanes = heads * PS
    width = lanes + 2 * N
    b = pl.program_id(0)
    bounds = [scal[i] for i in range(2, scal.shape[0])]
    start = b * BLOCK

    @pl.when(b == 0)
    def _():
        me = scal[0]
        load_blocks(xs, xv, me, BLOCK, sem_x)
        copies = load_blocks(ws, wv, me, ws[0].shape[0], sem_w, (0, 0, lanes))
        copies += load_blocks(wks, wv, me, ws[0].shape[0], sem_k, (lanes, 0, 2 * N + 128))
        load_blocks(ws, wg_o, me, ws[0].shape[0], sem_g, (0, lanes, lanes))
        cext[0:8, :] = jnp.zeros((8, width), F32)
        state[...] = jnp.zeros_like(state)
        for copy in copies:
            copy.wait()
        pltpu.make_async_copy(wv, w_o, sem_o).start()

    @pl.when(b == pl.num_programs(0) - 1)
    def _():
        rows = ws[0].shape[0]
        for k in range(n):
            to = wg_o.at[pl.ds(0, rows), pl.ds(0, lanes)]
            pltpu.make_async_copy(ws[k].at[:, pl.ds(lanes, lanes)], to, sem_g.at[k]).wait()
        pltpu.make_async_copy(wv, w_o, sem_o).wait()

    x = wait_block(xs[0], xv, scal[0], b, sem_x).astype(F32)
    scale = lax.rsqrt(jnp.mean(x * x, axis=1, keepdims=True) + EPS)
    normed = (x * scale * gain[...]).astype(BF)
    normed_o[...] = normed
    normed_t_o[...] = normed.T
    proj = dot(normed, wv[...]).astype(BF)
    conv_o[...] = proj[:, :lanes]
    convk_o[...] = proj[:, lanes:width]
    raw = pltpu.roll(proj[:, width:].astype(F32), 128 - scal[0] * own_heads, 1)
    raw_o[...] = raw
    cext[8:, :] = proj[:, :width].astype(F32)
    pre, _ = conv_forward(cext, taps, bounds, start)
    cext[0:8, :] = cext[BLOCK:, :]
    act = pre * sigmoid(pre)
    low = act.astype(BF)
    full = act[:, :lanes]
    keys, query = low[:, lanes : lanes + N], low[:, lanes + N :]
    _, step, _, cum, bias, enter, end, keep = scan_terms(raw, hp, bounds, start)
    cum_t, step_t = cum.T, step.T
    gram = dot_nt(query, keys)
    start_state = state[...]
    start_o[0] = start_state
    inter = dot_nt(query, start_state.astype(BF)) * expand(enter, heads // 2)
    weighted = (full * expand(end * step, heads // 2)).astype(BF)
    state[...] = head_rows(keep, lanes) * start_state + dot_tn(weighted, keys)
    rest = inter + skip[...] * full
    first = iota((BLOCK, 2 * PS), 1) < PS
    for p in range(heads // 2):
        at = slice(2 * PS * p, 2 * PS * (p + 1))
        pair = low[:, at]
        halves = (jnp.where(first, pair, 0), jnp.where(first, 0, pair))
        for t in range(2):
            rows, cols = slice(128 * t, 128 * (t + 1)), slice(0, 128 * (t + 1))
            total = rest[rows, at]
            for i in range(2):
                h = 2 * p + i
                decay = jnp.exp(cum[rows, h : h + 1] - cum_t[h : h + 1, cols] + bias[rows, cols])
                weights = (gram[rows, cols] * decay * step_t[h : h + 1, cols]).astype(BF)
                total = total + dot(weights, halves[i][cols, :])
            mixer_o[rows, at] = total


def gate_kernel(n, scal, *refs):
    gs = refs[:n]
    wv, normed, mixer, wo, gain, raw_o, stat_o, gv, sem_g = refs[n:]
    b = pl.program_id(0)

    @pl.when(b == 0)
    def _():
        load_blocks(gs, gv, scal[0], BLOCK, sem_g)

    raw = dot(normed[...], wv[...]).astype(BF)
    raw_o[...] = raw
    gate = raw.astype(F32)
    gated = mixer[...] * (gate * sigmoid(gate))
    g = wait_block(gs[0], gv, scal[0], b, sem_g)
    gno = dot_nt(g, wo[...])
    first = jnp.sum(gated * gated, axis=1, keepdims=True)
    second = jnp.sum(gno * gain[...] * gated, axis=1, keepdims=True)
    lane = iota((BLOCK, 128), 1)
    both = jnp.where(lane == 0, first, jnp.where(lane == 1, second, 0.0))
    stat_o[...] = both.T[0:8, :]


def output_kernel(n, nd, inner, scal, *refs):
    gs = refs[:n]
    stats = refs[n : 2 * n]
    normed_t, mixer, raw, wo, gain = refs[2 * n : 2 * n + 5]
    out_o, gssm_o, ggr_o, early_o = refs[2 * n + 5 : 2 * n + 9]
    gv, acc_o, acc_g, sem_g = refs[2 * n + 9 :]
    b = pl.program_id(0)

    @pl.when(b == 0)
    def _():
        load_blocks(gs, gv, scal[0], BLOCK, sem_g)
        acc_o[...] = jnp.zeros_like(acc_o)
        acc_g[...] = jnp.zeros_like(acc_g)

    stat = functools.reduce(lambda a, c: a + c, [s[...] for s in stats])
    stat = jnp.concatenate([stat, jnp.zeros((120, BLOCK), F32)], axis=0).T
    scale = lax.rsqrt(stat[:, 0:1] * (1.0 / inner) + EPS)
    mean = stat[:, 1:2] * (1.0 / inner)
    mix = mixer[...]
    gate = raw[...].astype(F32)
    sig = sigmoid(gate)
    act = gate * sig
    gated = mix * act
    normed_out = (gated * scale * gain[...]).astype(BF)
    g = wait_block(gs[0], gv, scal[0], b, sem_g)
    out_o[0] = dot(normed_out, wo[...]).astype(BF)
    acc_o[...] += dot_tn(normed_out, g)
    grad_gated = scale * (dot_nt(g, wo[...]) * gain[...] - gated * (mean * scale * scale))
    grad_raw = (grad_gated * mix * (sig * (1.0 + gate * (1.0 - sig)))).astype(BF)
    ggr_o[...] = grad_raw
    gssm_o[...] = (grad_gated * act).astype(BF)
    acc_g[...] += dot(normed_t[...], grad_raw)

    @pl.when(b == pl.num_programs(0) - 1)
    def _():
        share, lanes, model = acc_o.shape[0] // nd, acc_g.shape[1], acc_o.shape[1]
        rows = model // n
        part, side = rows // nd, max(1, model // lanes)
        for d in range(nd):
            to = d ^ scal[1] if nd > 1 else d
            early_o[to, 0:share, :] = acc_o[d * share : (d + 1) * share, :].astype(BF)
            for j in range(n):
                k = j ^ scal[0]
                first = pl.multiple_of(share + k // side * part, 8)
                value = acc_g[j * rows + d * part : j * rows + (d + 1) * part, :].astype(BF)
                for c in range(side):

                    @pl.when(k % side == c)
                    def _(c=c, value=value, first=first, to=to):
                        early_o[to, pl.ds(first, part), c * lanes : (c + 1) * lanes] = value


def store_shares(acc, out, n, nd, scal):
    rows = acc.shape[0] // n
    share = rows // nd
    for j in range(n):
        for d in range(nd):
            at = j * rows + d * share
            out[j ^ scal[0], d ^ scal[1] if nd > 1 else d] = acc[at : at + share, :].astype(BF)


def scan_kernel(n, nd, heads, own_heads, scal, *refs):
    normed_t, conv, conv_before, convk, convk_before, raw, starts, gssm, taps, hp, skip = refs[:11]
    proj_o, dw_o, small_o = refs[11:14]
    cexts, gexts, end_grad, acc, ggrams, ghts = refs[14:]
    lanes = heads * PS
    width = lanes + 2 * N
    i = pl.program_id(0)
    group = pl.num_programs(0) - 1 - i
    bounds = [scal[k] for k in range(2, scal.shape[0])]
    pairs = heads // 2
    later_of, conv_of = {}, {}

    @pl.when(i == 0)
    def _():
        gexts[0, 0:8, :] = jnp.zeros((8, width), F32)
        end_grad[...] = jnp.zeros_like(end_grad)
        acc[...] = jnp.zeros_like(acc)
        small_o[...] = jnp.zeros_like(small_o)

    def one(u):
        here = slice(u * BLOCK, (u + 1) * BLOCK)
        start = (group * PAIR + u) * BLOCK
        cext, gext, ggram, ght = (ref.at[u] for ref in (cexts, gexts, ggrams, ghts))
        for source, halo, at in ((conv, conv_before, slice(0, lanes)), (convk, convk_before, slice(lanes, width))):
            if u == 0:
                cext[0:8, at] = jnp.where(start > 0, halo[8:16, :].astype(F32), 0.0)
            else:
                cext[0:8, at] = source[u * BLOCK - 16 : u * BLOCK, :].astype(F32)[8:16, :]
            cext[8:, at] = source[here, :].astype(F32)
        pre, masks = conv_forward(cext, taps, bounds, start)
        sig = sigmoid(pre)
        act = pre * sig
        low = act.astype(BF)
        full = act[:, :lanes]
        keys, query = low[:, lanes : lanes + N], low[:, lanes + N :]
        z, step, rate, cum, bias, enter, end, keep = scan_terms(raw[here, :], hp, bounds, start)
        cum_t, step_t, enter_t = cum.T, step.T, enter.T
        yield
        gram = dot_nt(query, keys)
        grad = gssm[here, :]
        grad_f = grad.astype(F32)
        grad_t = grad_f.T.astype(BF)
        geared = jnp.concatenate(
            [grad_t[PS * h : PS * (h + 1), :].astype(F32) * enter_t[h : h + 1, :] for h in range(heads)],
            axis=0,
        ).astype(BF)
        later = end_grad[...] if u == PAIR - 1 else later_of[u + 1]
        later_of[u] = head_rows(keep, lanes) * later + dot(geared, query)
        yield
        first = iota((BLOCK, 2 * PS), 1) < PS
        lane = iota((128, 128), 1)
        row_totals = [jnp.zeros((128, 128), F32), jnp.zeros((128, 128), F32)]
        col_totals = []
        ggram[...] = jnp.zeros_like(ggram)
        for p in range(pairs):
            at = slice(2 * PS * p, 2 * PS * (p + 1))
            pair = low[:, at]
            halves = (jnp.where(first, pair, 0), jnp.where(first, 0, pair))
            for k in range(2):
                h = 2 * p + k
                own = slice(PS * h, PS * (h + 1))
                cols_total = None
                for t in range(2):
                    rows, cols = slice(128 * t, 128 * (t + 1)), slice(0, 128 * (t + 1))
                    decay = jnp.exp(cum[rows, h : h + 1] - cum_t[h : h + 1, cols] + bias[rows, cols])
                    table = dot_nt(grad[rows, at], halves[k][cols, :])
                    gram_here = gram[rows, cols]
                    step_row = step_t[h : h + 1, cols]
                    weights = (gram_here * decay * step_row).astype(BF)
                    common = table * decay
                    stepped = common * step_row
                    ggram[rows, cols] += stepped
                    col = jnp.sum(common * gram_here, axis=0, keepdims=True)
                    total = jnp.sum(stepped * gram_here, axis=1, keepdims=True)
                    row_totals[t] = jnp.where(lane == h, total, row_totals[t])
                    part = dot(grad_t[own, rows], weights)
                    if t == 0:
                        ght[own, 0:128] = part
                        cols_total = col
                    else:
                        ght[own, 0:128] += part[:, 0:128]
                        ght[own, 128:256] = part[:, 128:256]
                        cols_total = col + jnp.concatenate(
                            [cols_total, jnp.zeros((1, 128), F32)], axis=1
                        )
                col_totals.append(cols_total)
                yield
        col_totals.append(jnp.zeros((128 - heads, BLOCK), F32))
        grad_step = jnp.concatenate(col_totals, axis=0).T
        grad_cum = jnp.concatenate(row_totals, axis=0) - step * grad_step
        gg = ggram[...].astype(BF)
        start_state = starts[u]
        start_low = start_state.astype(BF)
        grad_cum += head_sum(grad_f * dot_nt(query, start_low)) * enter
        entered = (grad_f * expand(enter, pairs)).astype(BF)
        grad_query = dot(gg, keys) + dot(entered, start_low)
        end_low = later.astype(BF)
        scaled = end * step
        scaled_wide = expand(scaled, pairs)
        weighted = (full * scaled_wide).astype(BF)
        grad_weighted = dot_nt(keys, end_low)
        grad_keys = dot_tn(gg, query) + dot(weighted, end_low)
        grad_end = head_sum(grad_weighted * full)
        grad_step += grad_end * end
        end_terms = grad_end * scaled
        yield
        ones = jnp.ones((8, N), BF)
        held = sum(dot_nt(ones, part) for part in pieces(later * start_state, 2))
        grad_tail = jnp.sum(end_terms, axis=0, keepdims=True) + head_sum(held)[0:1, :] * keep
        final = iota((BLOCK, 1), 0) == BLOCK - 1
        grad_cum = grad_cum - end_terms + jnp.where(final, grad_tail, 0.0)
        upper = (iota((BLOCK, BLOCK), 0) <= iota((BLOCK, BLOCK), 1)).astype(BF)
        grad_log = sum(dot(upper, part) for part in pieces(grad_cum, 3))
        grad_step += grad_log * rate
        grad_rate = jnp.sum(grad_log * step, axis=0, keepdims=True)
        grad_heads = ght[...].T + grad_weighted * scaled_wide + grad_f * skip[...]
        grad_skip = jnp.sum(grad_f * full, axis=0, keepdims=True)
        yield
        grad_act = jnp.concatenate([grad_heads, grad_keys, grad_query], axis=1)
        grad_pre = grad_act * (sig * (1.0 + pre * (1.0 - sig)))
        gext[BLOCK:, :] = gexts[0, 0:8, :] if u == PAIR - 1 else gexts[u + 1, 0:8, :]
        conv_low = conv_backward(grad_pre, gext, cext, masks, taps, bounds, start, small_o).astype(BF)
        grad_raw = grad_step * sigmoid(z)
        small_o[0:1, width : width + 128] += jnp.sum(grad_raw, axis=0, keepdims=True)
        small_o[1:2, width : width + 128] += grad_rate * rate
        small_o[2:3, width : width + 128] += head_sum(jnp.broadcast_to(grad_skip, (8, lanes)))[0:1, :]
        raw_low = grad_raw.astype(BF)
        small_o[:, width + 128 :] += dot_nt(raw_low.T[0:16, :], normed_t[:, here])[0:8, :]
        conv_of[u] = conv_low
        proj_o[here, :width] = conv_low
        proj_o[here, width:] = pltpu.roll(grad_raw, scal[0] * own_heads, 1).astype(BF)

    running = [one(u) for u in reversed(range(PAIR))]
    while running:
        running = [block for block in running if next(block, True) is None]
    end_grad[...] = later_of[0]
    acc[...] += dot(normed_t[...], jnp.concatenate([conv_of[u] for u in range(PAIR)], axis=0))

    @pl.when(i == pl.num_programs(0) - 1)
    def _():
        store_shares(acc, dw_o, n, nd, scal)


def conv_backward(grad_pre, gext, cext, masks, taps, bounds, start, small_o):
    count = grad_pre.shape[1]
    gext[0:BLOCK, :] = grad_pre
    position = start + iota((BLOCK, 1), 0)
    left = document_end(bounds, position) - position
    total = None
    for k in range(KCONV):
        back = KCONV - 1 - k
        taken = cext[pl.ds(8 - back, BLOCK), :]
        after = gext[pl.ds(back, BLOCK), :]
        if back:
            taken = taken * masks[k]
            after = after * jnp.where(left > back, 1.0, 0.0)
        small_o[k : k + 1, 0:count] += jnp.sum(grad_pre * taken, axis=0, keepdims=True)
        term = taps[k : k + 1, :] * after
        total = term if total is None else total + term
    small_o[4:5, 0:count] += jnp.sum(grad_pre, axis=0, keepdims=True)
    return total


def normed_kernel(scal, proj, ggr, wv, wgv, gn_o):
    gn_o[0] = (dot_nt(proj[...], wv[...]) + dot_nt(ggr[...], wgv[...])).astype(BF)


def rows_dot(value, weight):
    product = value * weight.astype(F32)
    ones = jnp.ones((8, product.shape[1]), BF)
    return sum(dot_nt(ones, part) for part in pieces(product, 2))


def weights_kernel(n, own, order, scal, *refs):
    late, step, weight, gain, out, gain_o = refs
    rows, lanes = late.shape[1], (late.shape[2] - 2 * N) // (2 * n)
    me = scal[0]
    at = [
        0 if len(order) == 1 else pl.multiple_of((place ^ scal[1]) * rows, 8) for place in order
    ]

    def put(first):
        for e in range(len(order)):
            for k in range(n):
                for c in range(2):
                    from_lane = (2 * k + c) * lanes
                    value = late[e, :, from_lane : from_lane + own].astype(F32)
                    out[pl.ds(at[e], rows), pl.ds(c * DI + first(k), own)] = value

    if own % 128 == 0:
        put(lambda k: pl.multiple_of((me ^ k) * own, 128))
    else:
        for q in range(n):
            pl.when(me == q)(functools.partial(put, lambda k, q=q: (q ^ k) * own))
    for e in range(len(order)):
        out[pl.ds(at[e], rows), 2 * DI : 2 * DI + 2 * N] = late[e, :, late.shape[2] - 2 * N :].astype(F32)
    out[:, 2 * DI + 2 * N :] = step[:, :H]
    gain_o[...] = rows_dot(out[...], weight[...]) / gain[...]


def small_kernel(n, own_heads, scal, *refs):
    parts, (conv_o, step_o, heads_o), wide = refs[:n], refs[n : n + 3], refs[n + 3]
    own, rows = own_heads * PS, step_o.shape[0]
    lanes = own + own % 128
    width, chans = lanes + 2 * N, conv_o.shape[1]
    me = scal[0]
    for q in range(n):

        @pl.when(me == q)
        def _(q=q):
            shared, steps = jnp.zeros((8, 2 * N), F32), []
            for j in range(n):
                part = parts[q ^ j]
                wide[:, j * own : (j + 1) * own] = part[:, 0:own]
                shared = shared + part[:, lanes:width]
                first = width + 128 + q * rows
                steps.append(part[0:own_heads, first : first + rows])
            wide[:, DI:] = shared
            conv_o[...] = wide[:, q * chans : (q + 1) * chans]
            steps.append(jnp.zeros((128 - n * own_heads, rows), F32))
            step_o[...] = jnp.concatenate(steps, axis=0).T

    heads_o[...] = parts[0][:, width : width + 128]


def out_weight_kernel(order, scal, share, weight, gain, out, gain_o):
    rows = share.shape[1]
    for e, place in enumerate(order):
        at = 0 if len(order) == 1 else pl.multiple_of((place ^ scal[1]) * rows, 8)
        out[pl.ds(at, rows), :] = share[e].astype(F32)
    gain_o[...] = rows_dot(out[...], weight[...]) / gain[...]


def params_kernel(n, own_heads, scal, *refs):
    parts, (gain_o, taps_o, wide) = refs[:n], refs[n:]
    own = own_heads * PS
    lanes, chans, rows = own + own % 128, CONVCH // n, gain_o.shape[1] // n
    for q in range(n):

        @pl.when(scal[0] == q)
        def _(q=q):
            for j in range(n):
                part = parts[q ^ j][...].astype(F32)
                gain_o[:, j * rows : (j + 1) * rows] = part[0:1, 0:rows]
                wide[:, j * chans : (j + 1) * chans] = part[:, 0:chans]
            taps_o[...] = jnp.zeros(taps_o.shape, F32)
            for to, at, size in ((0, q * own, own), (lanes, DI, 2 * N)):
                taps_o[0:KCONV, to : to + size] = wide[2 : 2 + KCONV, at : at + size]
                taps_o[KCONV : KCONV + 1, to : to + size] = wide[1:2, at : at + size]


def packets_kernel(n, own, scal, weight, *outs):
    for k in range(n):
        first = pl.multiple_of((scal[0] ^ k) * own, 128)
        outs[k][:, 0:own] = weight[:, pl.ds(DI + first, own)]
        outs[k][:, own:] = weight[:, pl.ds(first, own)]
    shared = outs[n]
    shared[:, 0 : 2 * N] = weight[:, 2 * DI : 2 * DI + 2 * N]
    shared[:, 2 * N :] = jnp.zeros((shared.shape[0], 128), BF)
    shared[:, 2 * N : 2 * N + H] = weight[:, 2 * DI + 2 * N :]


def xor(value, axis, k):
    return lax.ppermute(value, axis, [(s, s ^ k) for s in range(lax.axis_size(axis))])


def gather_xor(value, axis):
    out = [value]
    for k in range(1, lax.axis_size(axis)):
        out.append(xor(value, axis, k) if k % 2 == 0 or k == 1 else xor(out[k - 1], axis, 1))
    return out


def by_owner(parts, me):
    stacked = jnp.stack(parts)
    return [lax.dynamic_index_in_dim(stacked, me ^ j, 0, False) for j in range(len(parts))]


def stages(count):
    out, low = [], 0
    bits = count.bit_length() - 1
    while low < bits:
        take = 1 if low == 0 else min(2, bits - low)
        out.append((low, take))
        low += take
    return out


def gather_order(count):
    order = [0]
    for low, take in reversed(stages(count)):
        order = [o | (m << low) for m in range(1 << take) for o in order]
    return order


class Shares:
    def __init__(self, value, dim):
        self.value, self.dim = value, dim
        self.low = [low for low, _ in stages(value.shape[dim])]
        self.bits = dict(stages(value.shape[dim]))
        sizes = [1 << self.bits[low] for low in reversed(self.low)]
        self.value = value.reshape(value.shape[:dim] + tuple(sizes) + value.shape[dim + 1 :])
        self.left = list(reversed(self.low))

    def reduce(self, low):
        at = self.dim + self.left.index(low)
        take = lambda m: lax.index_in_dim(self.value, m, at, False)
        recv = [xor(take(m), "dp", m << low) for m in range(1, 1 << self.bits[low])]
        total = take(0).astype(F32)
        for part in recv:
            total = total + part.astype(F32)
        self.value = total.astype(BF)
        self.left.remove(low)


def gather_step(value, low, take):
    return jnp.concatenate([value] + [xor(value, "dp", m << low) for m in range(1, 1 << take)], 0)


def pair_step(value, hop):
    return jnp.concatenate([value, xor(value, "dp", hop)], 0)


def pair_order(count):
    order = [0]
    bits = [1 << bit for bit in range(count.bit_length() - 1)]
    for hop in bits[1:][::-1] + bits[:1]:
        order += [place | hop for place in order]
    return order


def tie(*values):
    return lax.optimization_barrier(values)


def call(
    kernel, name, grid, scal, in_specs, args, out_specs, out_shape, scratch, flops, bytes_, aliases={}
):
    return pl.pallas_call(
        kernel,
        grid_spec=pltpu.PrefetchScalarGridSpec(
            num_scalar_prefetch=1,
            grid=grid,
            in_specs=in_specs,
            out_specs=out_specs,
            scratch_shapes=scratch,
        ),
        out_shape=out_shape,
        name=name,
        input_output_aliases=aliases,
        compiler_params=pltpu.CompilerParams(vmem_limit_bytes=LIMITS.get(name, VMEM_LIMIT)),
        cost_estimate=pl.CostEstimate(flops=flops, bytes_accessed=bytes_, transcendentals=0),
    )(scal, *args)


def local(
    block_input,
    out_cotangent,
    doc_lengths,
    norm_gain,
    in_weight,
    conv_weight,
    conv_bias,
    step_bias,
    decay_log,
    skip_gain,
    out_gain,
    out_weight,
):
    n, ndp = lax.axis_size("fsdp"), lax.axis_size("dp")
    me, dpi = lax.axis_index("fsdp"), lax.axis_index("dp")
    _, toks, model = block_input.shape
    length = toks * n
    nb = length // BLOCK
    own_heads = H // n
    heads = own_heads + own_heads % 2
    own, lanes = own_heads * PS, heads * PS
    width = lanes + 2 * N
    rows = model // n
    share = rows // ndp
    nd = ndp if share % 8 == 0 else 1
    x_own, g_own = block_input[0], out_cotangent[0]
    bounds = jnp.cumsum(doc_lengths[0])[:-1].astype(jnp.int32)
    scal = jnp.concatenate([jnp.stack([me, dpi]).astype(jnp.int32), bounds])

    def exchange(mine):
        return [mine[0]] + [xor(mine[k], "fsdp", k) for k in range(1, n)]

    xs = gather_xor(x_own, "fsdp")
    xs[1], packed_weight = tie(xs[1], in_weight)
    if own % 128 == 0:
        packets = call(
            functools.partial(packets_kernel, n, own),
            "packets",
            (1,),
            scal,
            [pl.BlockSpec(in_weight.shape, lambda b, s: (0, 0))],
            (packed_weight,),
            [pl.BlockSpec((rows, 2 * own), lambda b, s: (0, 0))] * n
            + [pl.BlockSpec((rows, 2 * N + 128), lambda b, s: (0, 0))],
            [jax.ShapeDtypeStruct((rows, 2 * own), BF)] * n
            + [jax.ShapeDtypeStruct((rows, 2 * N + 128), BF)],
            [],
            10**6,
            3 * 10**6,
        )
        own_cols, shared = list(packets[:n]), packets[-1]
    else:

        def columns(first):
            part = in_weight[:, first : first + DI].reshape(rows, n, own).transpose(1, 0, 2)
            part = jnp.pad(part, ((0, 0), (0, 0), (0, lanes - own)))
            return [lax.dynamic_index_in_dim(part, me ^ k, 0, False) for k in range(n)]

        own_cols = [jnp.concatenate(both, axis=1) for both in zip(columns(DI), columns(0))]
        shared = jnp.pad(in_weight[:, 2 * DI :], ((0, 0), (0, 128 - H)))
    chans = CONVCH // n
    pack = -(-max(rows, chans) // 128) * 128
    line = lambda value: jnp.pad(value, ((0, 0), (0, pack - value.shape[1])))
    small = jnp.concatenate(
        [line(norm_gain[None]), line(conv_bias[None]), line(conv_weight), jnp.zeros((2, pack), BF)]
    )
    xs[1], small = tie(xs[1], small)
    smalls = [small] + [xor(small, "fsdp", k) for k in range(1, n)]
    hp = jnp.stack([step_bias, decay_log]).astype(F32)
    hp = jnp.pad(hp, ((0, 6), (0, 128 - own_heads)))
    skip = jnp.pad(jnp.repeat(skip_gain.astype(F32), PS), (0, lanes - own)).reshape(1, lanes)

    out_w = jnp.pad(out_weight, ((0, lanes - own), (0, 0)))
    out_g = jnp.pad(out_gain.astype(F32), (0, lanes - own), constant_values=1.0).reshape(1, lanes)
    gain_row = norm_gain.astype(F32).reshape(1, rows)
    hp, skip, out_g, gain_row, scal, xs[2], *rest = tie(
        hp, skip, out_g, gain_row, scal, xs[2], *smalls[1:], *own_cols
    )
    smalls[1:], own_cols = rest[: n - 1], rest[n - 1 :]
    full = lambda *dims: pl.BlockSpec(dims, lambda b, s: (0,) * len(dims))
    gain_full, taps = call(
        functools.partial(params_kernel, n, own_heads),
        "params",
        (1,),
        scal,
        [full(8, pack)] * n,
        smalls,
        [full(1, model), full(8, width)],
        [jax.ShapeDtypeStruct((1, model), F32), jax.ShapeDtypeStruct((8, width), F32)],
        [pltpu.VMEM((8, CONVCH), F32)],
        10**6,
        10**5,
    )
    xs[3] = xor(xs[2], "fsdp", 1)
    wks = gather_xor(shared, "fsdp")
    ws = exchange(own_cols)
    g_tied, *_ = tie(g_own, *ws[1:])
    gs = gather_xor(g_tied, "fsdp")

    any_spec = pl.BlockSpec(memory_space=ANY)

    def whole(*shape):
        return pl.BlockSpec(shape, lambda b, s: (0,) * len(shape))

    def tokens(cols):
        return pl.BlockSpec((BLOCK, cols), lambda b, s: (b, 0))

    shape = jax.ShapeDtypeStruct
    normed, normed_t, conv_in, convk_in, raw_step, mixer, starts, w_conv, w_gate = call(
        functools.partial(forward_kernel, n, heads, own_heads),
        "forward",
        (nb,),
        scal,
        [any_spec] * (3 * n) + [whole(1, model), whole(8, width), whole(8, 128), whole(1, lanes)],
        (*xs, *ws, *wks, gain_full, taps, hp, skip),
        [
            tokens(model),
            pl.BlockSpec((model, BLOCK), lambda b, s: (0, b)),
            tokens(lanes),
            tokens(2 * N),
            tokens(128),
            tokens(lanes),
            pl.BlockSpec((1, lanes, N), lambda b, s: (b, 0, 0)),
            any_spec,
            any_spec,
        ],
        [
            shape((length, model), BF),
            shape((model, length), BF),
            shape((length, lanes), BF),
            shape((length, 2 * N), BF),
            shape((length, 128), F32),
            shape((length, lanes), F32),
            shape((nb, lanes, N), F32),
            shape((model, width + 128), BF),
            shape((model, lanes), BF),
        ],
        [
            pltpu.VMEM((length, model), BF),
            pltpu.VMEM((model, width + 128), BF),
            pltpu.VMEM((8 + BLOCK, width), F32),
            pltpu.VMEM((lanes, N), F32),
            pltpu.SemaphoreType.DMA,
            pltpu.SemaphoreType.DMA((n,)),
            pltpu.SemaphoreType.DMA((n,)),
            pltpu.SemaphoreType.DMA((n,)),
            pltpu.SemaphoreType.DMA((n,)),
        ],
        9 * 10**9,
        10**7,
    )

    gs[2], normed = tie(gs[2], normed)
    gs[3::2] = [xor(value, "fsdp", 1) for value in gs[2::2]]
    raw_gate, stat = call(
        functools.partial(gate_kernel, n),
        "gate",
        (nb,),
        scal,
        [any_spec] * n
        + [whole(model, lanes), tokens(model), tokens(lanes), whole(lanes, model), whole(1, lanes)],
        (*gs, w_gate, normed, mixer, out_w, out_g),
        [tokens(lanes), pl.BlockSpec((8, BLOCK), lambda b, s: (0, b))],
        [
            shape((length, lanes), BF),
            shape((8, length), F32),
        ],
        [
            pltpu.VMEM((length, model), BF),
            pltpu.SemaphoreType.DMA((n,)),
        ],
        2 * 10**9,
        10**7,
    )
    side = max(1, model // lanes)
    early_count = lanes // nd + -(-n // side) * (rows // nd)
    stats = [stat] + [xor(stat, "fsdp", k) for k in range(1, n)]

    out_part, gssm, ggr, early = call(
        functools.partial(output_kernel, n, nd, DI),
        "output",
        (nb,),
        scal,
        [any_spec] * n
        + [pl.BlockSpec((8, BLOCK), lambda b, s: (0, b))] * n
        + [pl.BlockSpec((model, BLOCK), lambda b, s: (0, b))]
        + [tokens(lanes), tokens(lanes)]
        + [whole(lanes, model), whole(1, lanes)],
        (*gs, *stats, normed_t, mixer, raw_gate, out_w, out_g),
        [
            pl.BlockSpec((1, BLOCK, model), lambda b, s: (b ^ s[0], 0, 0)),
            tokens(lanes),
            tokens(lanes),
            whole(nd, early_count, model),
        ],
        [
            shape((nb, BLOCK, model), BF),
            shape((length, lanes), BF),
            shape((length, lanes), BF),
            shape((nd, early_count, model), BF),
        ],
        [
            pltpu.VMEM((length, model), BF),
            pltpu.VMEM((lanes, model), F32),
            pltpu.VMEM((model, lanes), F32),
            pltpu.SemaphoreType.DMA((n,)),
        ],
        3 * 10**9,
        10**7,
    )

    def core_sum(parts):
        paired = parts.reshape(n // 2, 2, BLOCK, model)
        other = xor(paired[:, 1], "fsdp", 1)
        return (paired[:, 0].astype(F32) + other.astype(F32)).astype(BF)

    def chip_exchange(both):
        return both[0], [xor(both[k // 2], "fsdp", k) for k in range(2, n, 2)]

    def total_of(mine, recv):
        return functools.reduce(lambda a, c: a + c.astype(F32), recv, mine.astype(F32))

    def to_owners(shares):
        return [shares[0]] + [xor(shares[k], "fsdp", k) for k in range(1, n)]

    def late_rows(parts):
        shared_sum = functools.reduce(
            lambda a, c: a + c, [part[:, 2 * lanes :].astype(F32) for part in parts]
        )
        return jnp.concatenate(
            [part[:, : 2 * lanes] for part in parts] + [shared_sum.astype(BF)], axis=1
        )

    order = gather_order(ndp) if nd > 1 else [0]

    def step_rows_back(cols):
        return pl.BlockSpec((PAIR * BLOCK, cols), lambda b, s: (nb // PAIR - 1 - b, 0))

    def step_halo_back(cols):
        strips = PAIR * BLOCK // 16
        return pl.BlockSpec(
            (16, cols), lambda b, s: (jnp.maximum((nb // PAIR - 1 - b) * strips - 1, 0), 0)
        )

    if nd > 1:
        early = Shares(early, 0)
        early.reduce(0)
    out_sum = core_sum(out_part)

    proj_low, dw, small_grads = call(
        functools.partial(scan_kernel, n, nd, heads, own_heads),
        "scan_back",
        (nb // PAIR,),
        scal,
        [
            pl.BlockSpec((model, PAIR * BLOCK), lambda b, s: (0, nb // PAIR - 1 - b)),
            step_rows_back(lanes),
            step_halo_back(lanes),
            step_rows_back(2 * N),
            step_halo_back(2 * N),
            step_rows_back(128),
            pl.BlockSpec((PAIR, lanes, N), lambda b, s: (nb // PAIR - 1 - b, 0, 0)),
            step_rows_back(lanes),
            whole(8, width),
            whole(8, 128),
            whole(1, lanes),
        ],
        (
            normed_t,
            conv_in,
            conv_in,
            convk_in,
            convk_in,
            raw_step,
            starts,
            gssm,
            taps,
            hp,
            skip,
        ),
        [
            step_rows_back(width + 128),
            whole(n, nd, rows // nd, width),
            whole(8, width + 128 + model),
        ],
        [
            shape((length, width + 128), BF),
            shape((n, nd, rows // nd, width), BF),
            shape((8, width + 128 + model), F32),
        ],
        [
            pltpu.VMEM((PAIR, 8 + BLOCK, width), F32),
            pltpu.VMEM((PAIR, BLOCK + 8, width), F32),
            pltpu.VMEM((lanes, N), F32),
            pltpu.VMEM((model, width), F32),
            pltpu.VMEM((PAIR, BLOCK, BLOCK), F32),
            pltpu.VMEM((PAIR, lanes, BLOCK), F32),
        ],
        20 * 10**9,
        10**7,
    )
    if nd > 1:
        proj_low, dw, small_grads, early.value, out_sum = tie(
            proj_low, dw, small_grads, early.value, out_sum
        )
        late = Shares(dw, 1)
        late.reduce(0)
        for low in early.low[1:]:
            early.reduce(low)
        bits = [1 << bit for bit in range(ndp.bit_length() - 1)]
        hops = bits[1:][::-1]
        small_grads = small_grads + xor(small_grads, "dp", bits[0])
    (gn_part,) = call(
        normed_kernel,
        "normed_grad",
        (nb,),
        scal,
        [tokens(width + 128), tokens(lanes), whole(model, width + 128), whole(model, lanes)],
        (proj_low, ggr, w_conv, w_gate),
        [pl.BlockSpec((1, BLOCK, model), lambda b, s: (b ^ s[0], 0, 0))],
        [shape((nb, BLOCK, model), BF)],
        [],
        5 * 10**9,
        10**7,
    )
    if nd > 1:
        gn_part, late.value, early.value, small_grads = tie(
            gn_part, late.value, early.value, small_grads
        )
        own_rows, part = lanes // nd, rows // nd
        wo, gates = early.value[:own_rows], early.value[own_rows:]
        for low in late.low[1:]:
            late.reduce(low)
        gn_sum = core_sum(gn_part)
        wo = pair_step(wo[None], hops[0])
        late.value, wo, small_grads, gn_sum = tie(late.value, wo, small_grads, gn_sum)
        owned = to_owners(
            [
                jnp.concatenate(
                    [
                        gates[k // side * part : (k // side + 1) * part, k % side * lanes :][:, :lanes],
                        late.value[k],
                    ],
                    axis=1,
                )
                for k in range(n)
            ]
        )
        for hop in hops[1:]:
            wo = pair_step(wo, hop)
        gn_mine, gn_recv = chip_exchange(gn_sum)
        late = late_rows(owned)
        late, wo, small_grads, out_sum = tie(late, wo, small_grads, out_sum)
        gather = list(reversed(stages(ndp)))
        late = gather_step(late[None], *gather[0])
        wo = pair_step(wo, bits[0])
        out_mine, out_recv = chip_exchange(out_sum)
        late, wo, small_grads, *gn_recv = tie(late, wo, small_grads, *gn_recv)
        for low, take in gather[1:]:
            late = gather_step(late, low, take)
        for hop in hops:
            small_grads = small_grads + xor(small_grads, "dp", hop)
        small_other = xor(small_grads, "fsdp", 1)
        small_parts = [small_grads, small_other]
        for k in range(2, n, 2):
            pair = xor(jnp.concatenate([small_grads, small_other], axis=1), "fsdp", k)
            small_parts += [pair[:, : small_grads.shape[1]], pair[:, small_grads.shape[1] :]]
    else:
        out_mine, out_recv = chip_exchange(out_sum)
        gn_mine, gn_recv = chip_exchange(core_sum(gn_part))
        gates = [
            early[0, lanes + k // side * rows : lanes + (k // side + 1) * rows, k % side * lanes :][
                :, :lanes
            ]
            for k in range(n)
        ]
        owned = [jnp.concatenate([gates[k], dw[k, 0]], axis=1) for k in range(n)]
        late = lax.psum(late_rows(to_owners(owned)), "dp")[None]
        wo = lax.psum(early[0, :lanes], "dp")[None]
        small_parts = to_owners([lax.psum(small_grads, "dp")] * n)
    block_output = (x_own.astype(F32) + total_of(out_mine, out_recv)).astype(BF)[None]
    total_in = total_of(gn_mine, gn_recv)
    inputs = x_own.astype(F32)
    scale_in = lax.rsqrt(jnp.mean(inputs * inputs, axis=-1, keepdims=True) + EPS)
    gained = total_in * gain_full
    input_grad = scale_in * (
        gained - inputs * jnp.mean(gained * inputs, axis=-1, keepdims=True) * scale_in * scale_in
    ) + g_own.astype(F32)
    input_grad = input_grad.astype(BF)[None]

    conv_grads, step_cols, head_grads = call(
        functools.partial(small_kernel, n, own_heads),
        "small_grads",
        (1,),
        scal,
        [whole(*part.shape) for part in small_parts],
        small_parts,
        [whole(8, chans), whole(rows, 128), whole(8, 128)],
        [shape((8, chans), F32), shape((rows, 128), F32), shape((8, 128), F32)],
        [pltpu.VMEM((8, CONVCH), F32)],
        10**6,
        10**6,
    )
    head_grads = head_grads[:3, :own_heads]

    grad_in, grad_gain = call(
        functools.partial(weights_kernel, n, own, order),
        "in_weight_grad",
        (1,),
        scal,
        [
            whole(*late.shape),
            whole(rows, 128),
            whole(*in_weight.shape),
            whole(1, rows),
        ],
        (late, step_cols, in_weight, gain_row),
        [whole(*in_weight.shape), whole(8, rows)],
        [shape(in_weight.shape, F32), shape((8, rows), F32)],
        [],
        10**8,
        6 * 10**6,
    )
    grad_out, grad_out_gain = call(
        functools.partial(out_weight_kernel, pair_order(ndp) if nd > 1 else [0]),
        "out_weight_grad",
        (1,),
        scal,
        [whole(*wo.shape), whole(lanes, model), whole(1, lanes)],
        (wo, out_w, out_g),
        [whole(lanes, model), whole(8, lanes)],
        [shape((lanes, model), F32), shape((8, lanes), F32)],
        [],
        10**8,
        3 * 10**6,
    )
    return (
        block_output,
        input_grad,
        grad_gain[0],
        grad_in,
        conv_grads[:KCONV],
        conv_grads[KCONV],
        head_grads[0],
        head_grads[1],
        head_grads[2],
        grad_out_gain[0, :own],
        grad_out[:own],
    )


def solution(mesh):
    return jax.shard_map(
        local,
        mesh=mesh,
        in_specs=(
            P("dp", "fsdp", None),
            P("dp", "fsdp", None),
            P("dp", None),
            P("fsdp"),
            P("fsdp", None),
            P(None, "fsdp"),
            P("fsdp"),
            P("fsdp"),
            P("fsdp"),
            P("fsdp"),
            P("fsdp"),
            P("fsdp", None),
        ),
        out_specs=(
            P("dp", "fsdp", None),
            P("dp", "fsdp", None),
            P("fsdp"),
            P("fsdp", None),
            P(None, "fsdp"),
            P("fsdp"),
            P("fsdp"),
            P("fsdp"),
            P("fsdp"),
            P("fsdp"),
            P("fsdp", None),
        ),
        check_vma=False,
    )
```
